1024 devices in a mesh: expert: 64 (over x, z), dp: 16 (over y, core).
Axes of the slice: x: 4, y: 8, z: 16, core: 2. Of those that a mesh axis runs over, the one named last changes fastest.
Arguments:
- latent: bfloat16 [131072, 1024], P(('expert', 'dp')), may hold values from -6 to 6
- cotangent: bfloat16 [131072, 1024], P(('expert', 'dp')), may hold values from -6 to 6
- routes: int32 [131072, 1], P(('expert', 'dp')), may hold values from 0 to 63; in each aligned block of 128 rows (0 to 127, 128 to 255, ...) at most 3 rows name the same one
- gates: float32 [131072, 1], P(('expert', 'dp')), may hold values from 0.25 to 1
- up_weight: bfloat16 [64, 1024, 2048], P('expert'), may hold values from -0.1875 to 0.1875
- down_weight: bfloat16 [64, 2048, 1024], P('expert'), may hold values from -0.125 to 0.125
Outputs:
- mixed: bfloat16 [131072, 1024], P(('expert', 'dp'))
- down_grad: bfloat16 [64, 2048, 1024], P('expert', 'dp')
The draws below stay inside these ranges and needn't reach their ends.
Inputs may be any that keep to these rules, and one draw needn't show every extreme that they name: `routes`: in each aligned block of 128 rows (the tokens of one device) no expert is named by more than 3 rows, and in some blocks one expert is named by exactly 3 rows.
All inputs are finite; a program needn't handle non-finite values.
Results may differ from the reference program's by a relative error of at most 0.019.
Values may be sent and summed in bfloat16 or wider, within the bound.
No kernel may reach another device: no remote copies, remote signals or barrier semaphores. Data moves between devices by JAX's collectives and lax.ppermute only.
A program may use at most 64 MiB of HBM per device.

```python
import math
import jax
import jax.numpy as jnp
import numpy as np
from jax import lax

L = 1024
H = 2048
TOK_DEV = 128
TOP = 1
EXPERTS = 64
CAP = 3
TOKENS = 131072
N_EXPERT = 64
N_DP = 16


def shard_levels(own_key, shape, shards, least, high):
    level = 1.0
    for dim, parts in shards:
        steps = jax.random.uniform(jax.random.fold_in(jax.random.fold_in(own_key, 6), dim), (parts,), jnp.float32, least / len(shards), high / len(shards))
        level = level * jnp.repeat(jnp.exp(steps), shape[dim] // parts).reshape((-1,) + (1,) * (len(shape) - 1 - dim))
    return level


def assign_block(rng, own, number, rows, number_of, top, limit, skew):
    sequence = jax.random.permutation(rng, number_of)
    packed, ordinary = load_shares(number_of, rows * top, limit, skew, True), load_shares(number_of, rows * top, limit, skew, False)
    places = jnp.arange(number_of)

    def named(tallies, rotation):
        used = int((tallies > 0).sum())
        fixed = max(1, used // 4)
        passed = fixed + (places - fixed + rotation * (used - fixed)) % max(1, number_of - fixed)
        return jnp.zeros((number_of,), jnp.int32).at[sequence[jnp.where(places < fixed, places, passed)]].set(jnp.asarray(tallies, jnp.int32))

    tallies = jnp.where(number % 4 == 0, named(packed, number // 4), named(ordinary, number - number // 4 - 1))
    mixed = jax.random.permutation(jax.random.fold_in(own, 3), number_of)
    source_of, taker = mixed[0:number_of // 2 * 2:2], mixed[1:number_of // 2 * 2:2]
    room = jnp.minimum(tallies[source_of] - 1, limit - tallies[taker]) // 2
    room = jnp.where((source_of == sequence[0]) | (taker == sequence[0]) | (tallies[taker] == 0), 0, jnp.maximum(room, 0))
    passed = jax.random.randint(jax.random.fold_in(own, 4), (number_of // 2,), 0, 1 << 20) % (room + 1)
    tallies = tallies.at[source_of].add(-passed).at[taker].add(passed)
    labels = jnp.searchsorted(jnp.cumsum(tallies), jnp.arange(rows * top), side="right").astype(jnp.int32)
    listing = labels.reshape(top, rows).T
    listing = listing[jax.random.permutation(jax.random.fold_in(own, 1), rows)]
    rotation = jax.random.randint(jax.random.fold_in(own, 2), (rows, 1), 0, top)
    return jnp.take_along_axis(listing, (jnp.arange(top)[None, :] + rotation) % top, axis=1)


def load_shares(amount, total, reach, lean, full):
    loads = [(1 << 20) // math.isqrt(rank ** lean) + 1 for rank in range(1, amount + 1)]
    largest = reach if full else min(reach, max(-(-total // amount), total * loads[0] // sum(loads)))
    least = 1 if total - largest >= amount - 1 else 0
    holding, rest = [largest] + [least] * (amount - 1), total - largest - least * (amount - 1)
    while rest > 0:
        movable = [i for i in range(1, amount) if holding[i] < largest] or [i for i in range(1, amount) if holding[i] < reach]
        mass, budget = sum([loads[i] for i in movable]), rest
        for i in movable:
            more = min(reach - holding[i], max(1, budget * loads[i] // mass), rest)
            holding[i] = holding[i] + more
            rest = rest - more
    return np.array(holding)


def scatter_about(key, shape, spread, limit, cuts=(), kind=jnp.bfloat16):
    result = jax.random.normal(key, shape, jnp.float32) * spread
    if len(cuts) > 0:
        result = shard_levels(key, shape, cuts, -0.22, 0.18) * result
    return jnp.clip(result, min=-limit, max=limit).astype(kind)


def setup_inputs(seed: int = 0) -> dict:
    key_list = jax.random.split(jax.random.key(seed), 7)
    latent = scatter_about(key_list[0], (TOKENS, L), 1.0, 6.0, ((0, 1024),))
    cotangent = scatter_about(key_list[1], (TOKENS, L), 1.0, 6.0, ((0, 1024),))
    routes_keys = jax.random.split(jax.random.fold_in(key_list[2], 1), TOKENS // TOK_DEV)
    routes_turns = jax.random.permutation(jax.random.fold_in(key_list[2], 3), TOKENS // TOK_DEV)
    routes = jax.vmap(lambda own, number: assign_block(jax.random.fold_in(key_list[2], 2), own, number, TOK_DEV, EXPERTS, TOP, CAP, 2))(routes_keys, routes_turns).reshape((TOKENS, TOP))
    gates = jnp.clip(0.25 + 0.75 * jax.random.uniform(key_list[3], (TOKENS, TOP), jnp.float32) ** shard_levels(key_list[3], (TOKENS, TOP), ((0, 1024),), -0.2, 0.2), 0.25, 1.0)
    up_weight = scatter_about(key_list[4], (EXPERTS, L, H), L ** -0.5, 0.1875, ((0, 64),))
    down_weight = scatter_about(key_list[5], (EXPERTS, H, L), H ** -0.5, 0.125, ((0, 64),))
    return dict(latent=latent, cotangent=cotangent, routes=routes, gates=gates, up_weight=up_weight, down_weight=down_weight)


def reference(latent, cotangent, routes, gates, up_weight, down_weight):
    slots = N_EXPERT * CAP
    key_total = EXPERTS * N_DP
    position = jnp.arange(TOKENS, dtype=jnp.int32)
    data_group = (position // TOK_DEV) % N_DP
    route = routes[:, 0].astype(jnp.int32)
    sort_key = (route * N_DP + data_group).astype(jnp.int32)
    order = jnp.argsort(sort_key, stable=True).astype(jnp.int32)
    counts = jax.ops.segment_sum(jnp.ones((TOKENS,), jnp.int32), sort_key, num_segments=key_total).astype(jnp.int32)
    starts = (jnp.cumsum(counts) - counts).astype(jnp.int32)
    gate = gates[:, 0]
    weighted = (gate[:, None] * cotangent.astype(jnp.float32)).astype(jnp.bfloat16)
    padding = jnp.zeros((slots, L), jnp.bfloat16)
    sorted_latent = jnp.concatenate([latent[order], padding], axis=0)
    sorted_weighted = jnp.concatenate([weighted[order], padding], axis=0)
    factor = 1.0 / (TOK_DEV * TOP * N_DP) ** 0.5
    ranks = jnp.arange(slots, dtype=jnp.int32)

    def one_expert(expert):
        up_matrix = up_weight[expert]
        down_matrix = down_weight[expert]

        def one_group(total, group_index):
            key_index = expert * N_DP + group_index
            start = starts[key_index]
            count = counts[key_index]
            live = (ranks < count)[:, None]
            rows_in = lax.dynamic_slice_in_dim(sorted_latent, start, slots, 0)
            rows_cot = lax.dynamic_slice_in_dim(sorted_weighted, start, slots, 0)
            rows_in = jnp.where(live, rows_in, jnp.zeros_like(rows_in))
            rows_cot = jnp.where(live, rows_cot, jnp.zeros_like(rows_cot))
            preact = jnp.dot(rows_in, up_matrix, preferred_element_type=jnp.float32)
            hidden = (jnp.maximum(preact, 0.0) ** 2).astype(jnp.bfloat16)
            expert_out = jnp.dot(hidden, down_matrix, preferred_element_type=jnp.float32).astype(jnp.bfloat16)
            product = lax.dot_general(hidden, rows_cot, (((0,), (0,)), ((), ())), preferred_element_type=jnp.float32)
            rounded = lax.optimization_barrier((factor * product).astype(jnp.bfloat16))
            return total + rounded.astype(jnp.float32), expert_out

        total, outputs = lax.scan(one_group, jnp.zeros((H, L), jnp.float32), jnp.arange(N_DP, dtype=jnp.int32))
        return outputs, total.astype(jnp.bfloat16)

    outputs, down_grad = lax.map(one_expert, jnp.arange(EXPERTS, dtype=jnp.int32))
    flat_out = outputs.reshape(key_total * slots, L)
    sorted_keys = sort_key[order]
    offsets = (jnp.arange(TOKENS, dtype=jnp.int32) - starts[sorted_keys]).astype(jnp.int32)
    sorted_out = flat_out[(sorted_keys * slots + offsets).astype(jnp.int32)]
    token_out = jnp.zeros((TOKENS, L), jnp.bfloat16).at[order].set(sorted_out)
    mixed = (gate[:, None] * token_out.astype(jnp.float32)).astype(jnp.bfloat16)
    return mixed, down_grad
```

```python
import functools

import jax
import jax.numpy as jnp
from jax import lax
from jax.experimental import pallas as pl
from jax.experimental.pallas import tpu as pltpu
from jax.sharding import Mesh, PartitionSpec as P

LANES = 128
CORES = 2
VMEM_LIMIT = 48 * 1024 * 1024


def slot_picks(routes_ref, experts, capacity):
    tokens = routes_ref.shape[1]
    named = routes_ref[...] == lax.broadcasted_iota(jnp.int32, (experts, tokens), 0)
    earlier = lax.broadcasted_iota(jnp.int32, (tokens, tokens), 0) < lax.broadcasted_iota(
        jnp.int32, (tokens, tokens), 1
    )
    rank = jnp.dot(
        jnp.where(named, 1.0, 0.0).astype(jnp.bfloat16),
        jnp.where(earlier, 1.0, 0.0).astype(jnp.bfloat16),
        preferred_element_type=jnp.float32,
    )
    return [
        jnp.where(jnp.logical_and(named, rank == float(k)), 1.0, 0.0) for k in range(capacity)
    ]


def pack_kernel(experts, capacity, routes_ref, gates_ref, latent_ref, cot_ref, out_ref, stage):
    chunks = latent_ref.shape[1] // LANES
    block = 2 * capacity * chunks
    for k, pick in enumerate(slot_picks(routes_ref, experts, capacity)):
        gate = jnp.sum(pick * gates_ref[...], axis=1, keepdims=True)
        pick = pick.astype(jnp.bfloat16)
        rows = jnp.dot(pick, latent_ref[...], preferred_element_type=jnp.float32)
        cots = jnp.dot(pick, cot_ref[...], preferred_element_type=jnp.float32) * gate
        for c in range(chunks):
            lanes = slice(c * LANES, (c + 1) * LANES)
            first = 2 * k * chunks + c
            stage[pl.ds(first, experts, stride=block), :] = rows[:, lanes]
            stage[pl.ds(first + chunks, experts, stride=block), :] = cots[:, lanes]
    out_ref[...] = stage[...].astype(jnp.bfloat16)


def unpack(stage, out_ref, at, sources, capacity, parts, part):
    chunks = out_ref.shape[1] // LANES
    block = parts * capacity * chunks
    for k in range(capacity):
        for c in range(chunks):
            out_ref[at + k * sources : at + (k + 1) * sources, c * LANES : (c + 1) * LANES] = stage[
                pl.ds((parts * k + part) * chunks + c, sources, stride=block), :
            ].astype(jnp.bfloat16)


def activation(rows, weight):
    preact = jnp.dot(rows, weight, preferred_element_type=jnp.float32)
    return (jnp.maximum(preact, 0.0) ** 2).astype(jnp.bfloat16)


def expert_kernel(
    sources, capacity, recv_ref, up_ref, down_ref, hidden_ref, cots_ref, out_ref, stage, rows
):
    width = rows.shape[1]
    chunks = width // LANES
    stage[...] = recv_ref[...].astype(jnp.float32)
    unpack(stage, rows, 0, sources, capacity, 2, 0)
    unpack(stage, cots_ref, 0, sources, capacity, 2, 1)
    tile = 2 * LANES

    @pl.loop(0, up_ref.shape[1] // tile)
    def _(j):
        columns = pl.ds(pl.multiple_of(j * tile, tile), tile)
        hidden_ref[:, columns] = activation(rows[...], up_ref[:, columns])

    for j in range(width // tile):
        out = jnp.dot(
            hidden_ref[...],
            down_ref[:, j * tile : (j + 1) * tile],
            preferred_element_type=jnp.float32,
        )
        for k in range(capacity):
            for c in range(tile // LANES):
                first = k * chunks + j * (tile // LANES) + c
                stage[pl.ds(first, sources, stride=capacity * chunks), :] = out[
                    k * sources : (k + 1) * sources, c * LANES : (c + 1) * LANES
                ]
    out_ref[...] = stage[: sources * capacity * chunks, :].astype(jnp.bfloat16)


def grad_kernel(
    sources,
    capacity,
    factor,
    core_ref,
    hidden_ref,
    own_cots_ref,
    other_ref,
    up_ref,
    part_ref,
    stage,
    rows,
    cots,
):
    me = core_ref[0]
    slots = sources * capacity
    stage[...] = other_ref[...].astype(jnp.float32)
    unpack(stage, rows, 0, sources, capacity, 2, 0)
    unpack(stage, cots, slots, sources, capacity, 2, 1)
    cots[:slots, :] = own_cots_ref[...]

    @pl.loop(0, part_ref.shape[0] // (2 * LANES))
    def _(y):
        blocks = [
            pl.ds(pl.multiple_of((CORES * (2 * y + i) + me) * LANES, LANES), LANES)
            for i in range(2)
        ]
        other = activation(
            rows[...], jnp.concatenate([up_ref[:, block] for block in blocks], axis=1)
        )
        own = jnp.concatenate([hidden_ref[:, block] for block in blocks], axis=1)
        product = lax.dot_general(
            jnp.concatenate([own, other], axis=0),
            cots[...],
            (((0,), (0,)), ((), ())),
            preferred_element_type=jnp.float32,
        )
        part_ref[pl.ds(pl.multiple_of(y * 2 * LANES, 2 * LANES), 2 * LANES), :] = (
            factor * product
        ).astype(jnp.bfloat16)


def mix_kernel(experts, capacity, routes_ref, gates_ref, back_ref, out_ref, stage):
    width = out_ref.shape[1]
    chunks = width // LANES
    block = capacity * chunks
    stage[...] = back_ref[...].astype(jnp.float32)
    picks = slot_picks(routes_ref, experts, capacity)
    gates = [jnp.sum(pick * gates_ref[...], axis=1, keepdims=True) for pick in picks]
    picks = jnp.concatenate(picks, axis=0).astype(jnp.bfloat16)
    for c in range(chunks):
        scaled = [
            (gates[k] * stage[pl.ds(k * chunks + c, experts, stride=block), :]).astype(jnp.bfloat16)
            for k in range(capacity)
        ]
        out_ref[:, c * LANES : (c + 1) * LANES] = lax.dot_general(
            picks,
            jnp.concatenate(scaled, axis=0),
            (((0,), (0,)), ((), ())),
            preferred_element_type=jnp.float32,
        ).astype(jnp.bfloat16)


def call(kernel, out_shape, scratch, flops, moved, smem=()):
    def spec(i):
        return pl.BlockSpec(memory_space=pltpu.SMEM if i in smem else pltpu.VMEM)

    def run(*args):
        return pl.pallas_call(
            kernel,
            out_shape=out_shape,
            in_specs=[spec(i) for i in range(len(args))],
            out_specs=jax.tree.map(lambda _: pl.BlockSpec(memory_space=pltpu.VMEM), out_shape),
            scratch_shapes=scratch,
            compiler_params=pltpu.CompilerParams(vmem_limit_bytes=VMEM_LIMIT),
            cost_estimate=pl.CostEstimate(flops=flops, bytes_accessed=moved, transcendentals=0),
        )(*args)

    return run


def on_device(latent, cotangent, routes, gates, up_weight, down_weight):
    experts = lax.axis_size("expert")
    groups = lax.axis_size("y") * lax.axis_size("core")
    tokens, width = latent.shape
    hidden_width = up_weight.shape[2]
    capacity = max(2, 3 * tokens // (2 * experts))
    slots = experts * capacity
    chunks = width // LANES
    factor = 1.0 / (tokens * groups) ** 0.5
    bf16 = functools.partial(jax.ShapeDtypeStruct, dtype=jnp.bfloat16)
    f32 = lambda *shape: pltpu.VMEM(shape, jnp.float32)
    half = lambda *shape: pltpu.VMEM(shape, jnp.bfloat16)
    route_row, gate_row = routes.reshape(1, tokens), gates.reshape(1, tokens)

    sent = call(
        functools.partial(pack_kernel, experts, capacity),
        bf16((2 * slots * chunks, LANES)),
        [f32(2 * slots * chunks, LANES)],
        4 * slots * tokens * width,
        4 * tokens * width + 4 * slots * width,
    )(route_row, gate_row, latent, cotangent)
    received = lax.all_to_all(
        sent.reshape(experts, -1, LANES), "expert", split_axis=0, concat_axis=0, tiled=True
    ).reshape(-1, LANES)
    other = lax.ppermute(received, "core", [(i, CORES - 1 - i) for i in range(CORES)])
    hidden, cots, out = call(
        functools.partial(expert_kernel, experts, capacity),
        (bf16((slots, hidden_width)), bf16((slots, width)), bf16((slots * chunks, LANES))),
        [f32(2 * slots * chunks, LANES), half(slots, width)],
        4 * slots * width * hidden_width,
        4 * width * hidden_width + 8 * slots * width + 2 * slots * hidden_width,
    )(received, up_weight[0], down_weight[0])
    core = lax.axis_index("core").astype(jnp.int32).reshape(1)
    share = hidden_width // CORES
    partial = call(
        functools.partial(grad_kernel, experts, capacity, factor),
        bf16((share, width)),
        [
            f32(2 * slots * chunks, LANES),
            half(slots, width),
            half(CORES * slots, width),
        ],
        3 * slots * width * hidden_width,
        2 * width * hidden_width + 6 * slots * width + 2 * share * width,
        smem=(0,),
    )(core, hidden, cots, other, up_weight[0])
    down_grad = lax.psum_scatter(partial, "y", scatter_dimension=0, tiled=True)
    returned = lax.all_to_all(
        out.reshape(experts, -1, LANES), "expert", split_axis=0, concat_axis=0, tiled=True
    ).reshape(-1, LANES)
    mixed = call(
        functools.partial(mix_kernel, experts, capacity),
        bf16((tokens, width)),
        [f32(slots * chunks, LANES)],
        2 * slots * tokens * width,
        2 * slots * width + 2 * tokens * width,
    )(route_row, gate_row, returned)
    return mixed, down_grad[None]


def solution(mesh):
    experts, groups = mesh.devices.shape
    split = Mesh(mesh.devices.reshape(experts, groups // CORES, CORES), ("expert", "y", "core"))
    rows = P(("expert", "y", "core"), None)
    weights = P("expert", None, None)
    return jax.shard_map(
        on_device,
        mesh=split,
        in_specs=(rows, rows, rows, rows, weights, weights),
        out_specs=(rows, P("expert", ("y", "core"), None)),
        check_vma=False,
    )
```

```python
import functools

import jax
import jax.numpy as jnp
from jax import lax
from jax.experimental import pallas as pl
from jax.experimental.pallas import tpu as pltpu
from jax.sharding import Mesh, PartitionSpec as P

LANES = 128
CORES = 2
VMEM_LIMIT = 48 * 1024 * 1024


def slot_picks(routes_ref, experts, capacity):
    tokens = routes_ref.shape[1]
    named = routes_ref[...] == lax.broadcasted_iota(jnp.int32, (experts, tokens), 0)
    earlier = lax.broadcasted_iota(jnp.int32, (tokens, tokens), 0) < lax.broadcasted_iota(
        jnp.int32, (tokens, tokens), 1
    )
    rank = jnp.dot(
        jnp.where(named, 1.0, 0.0).astype(jnp.bfloat16),
        jnp.where(earlier, 1.0, 0.0).astype(jnp.bfloat16),
        preferred_element_type=jnp.float32,
    )
    return [
        jnp.where(jnp.logical_and(named, rank == float(k)), 1.0, 0.0) for k in range(capacity)
    ]


def pack_kernel(
    experts, capacity, routes_hbm, gates_hbm, latent_hbm, cot_hbm, out_ref, stage, routes, gates, latent, cot, sems
):
    copies = [
        pltpu.make_async_copy(source, target, sems.at[i])
        for i, (source, target) in enumerate(
            ((routes_hbm, routes), (gates_hbm, gates), (latent_hbm, latent), (cot_hbm, cot))
        )
    ]
    for copy in copies:
        copy.start()
    chunks = latent.shape[1] // LANES
    block = 2 * capacity * chunks
    copies[0].wait()
    copies[1].wait()
    picks = slot_picks(routes, experts, capacity)
    for part, source in enumerate((latent, cot)):
        copies[2 + part].wait()
        for k, pick in enumerate(picks):
            rows = jnp.dot(
                pick.astype(jnp.bfloat16), source[...], preferred_element_type=jnp.float32
            )
            if part == 1:
                rows = rows * jnp.sum(pick * gates[...], axis=1, keepdims=True)
            for c in range(chunks):
                first = (2 * k + part) * chunks + c
                stage[pl.ds(first, experts, stride=block), :] = rows[:, c * LANES : (c + 1) * LANES]
    out_ref[...] = stage[...].astype(jnp.bfloat16)


def unpack(stage, out_ref, at, sources, capacity, parts, part):
    chunks = out_ref.shape[1] // LANES
    block = parts * capacity * chunks
    for k in range(capacity):
        for c in range(chunks):
            out_ref[at + k * sources : at + (k + 1) * sources, c * LANES : (c + 1) * LANES] = stage[
                pl.ds((parts * k + part) * chunks + c, sources, stride=block), :
            ].astype(jnp.bfloat16)


def activation(rows, weight):
    preact = jnp.dot(rows, weight, preferred_element_type=jnp.float32)
    return (jnp.maximum(preact, 0.0) ** 2).astype(jnp.bfloat16)


def hidden_kernel(
    sources, capacity, recv_ref, up_hbm, hidden_ref, cots_ref, stage, rows, up, sems
):
    tile = 2 * LANES
    tiles = up.shape[1] // tile

    def fetch(j):
        columns = pl.ds(pl.multiple_of(j * tile, tile), tile)
        return pltpu.make_async_copy(up_hbm.at[:, columns], up.at[:, columns], sems.at[j])

    for j in range(tiles):
        fetch(j).start()
    stage[...] = recv_ref[...].astype(jnp.float32)
    unpack(stage, rows, 0, sources, capacity, 2, 0)
    unpack(stage, cots_ref, 0, sources, capacity, 2, 1)

    @pl.loop(0, tiles)
    def _(j):
        fetch(j).wait()
        columns = pl.ds(pl.multiple_of(j * tile, tile), tile)
        hidden_ref[:, columns] = activation(rows[...], up[:, columns])


def grad_kernel(
    sources,
    capacity,
    factor,
    core_ref,
    hidden_ref,
    own_cots_ref,
    other_ref,
    up_hbm,
    part_hbm,
    stage,
    rows,
    cots,
    up,
    part,
    sems,
    out_sems,
):
    me = core_ref[0]
    slots = sources * capacity
    blocks = part.shape[0] // LANES

    def source_columns(y):
        return pl.ds(pl.multiple_of((CORES * y + me) * LANES, LANES), LANES)

    def fetch(y):
        return pltpu.make_async_copy(
            up_hbm.at[:, source_columns(y)],
            up.at[:, pl.ds(pl.multiple_of(y * LANES, LANES), LANES)],
            sems.at[y],
        )

    def flush(j):
        at = pl.ds(pl.multiple_of(j * 2 * LANES, 2 * LANES), 2 * LANES)
        return pltpu.make_async_copy(part.at[at, :], part_hbm.at[at, :], out_sems.at[j])

    for y in range(blocks):
        fetch(y).start()
    stage[...] = other_ref[...].astype(jnp.float32)
    unpack(stage, rows, 0, sources, capacity, 2, 0)
    unpack(stage, cots, slots, sources, capacity, 2, 1)
    cots[:slots, :] = own_cots_ref[...]

    @pl.loop(0, blocks // 2)
    def _(j):
        fetch(2 * j).wait()
        fetch(2 * j + 1).wait()
        at = pl.ds(pl.multiple_of(j * 2 * LANES, 2 * LANES), 2 * LANES)
        other = activation(rows[...], up[:, at])
        own = jnp.concatenate([hidden_ref[:, source_columns(2 * j + i)] for i in range(2)], axis=1)
        product = lax.dot_general(
            jnp.concatenate([own, other], axis=0),
            cots[...],
            (((0,), (0,)), ((), ())),
            preferred_element_type=jnp.float32,
        )
        part[at, :] = (factor * product).astype(jnp.bfloat16)
        flush(j).start()

    for j in range(blocks // 2):
        flush(j).wait()


def down_kernel(sources, capacity, hidden_ref, down_hbm, out_ref, stage, down, sems):
    width = down.shape[1]
    chunks = width // LANES
    tile = 2 * LANES
    copies = [
        pltpu.make_async_copy(
            down_hbm.at[:, pl.ds(j * tile, tile)], down.at[:, pl.ds(j * tile, tile)], sems.at[j]
        )
        for j in range(width // tile)
    ]
    for copy in copies:
        copy.start()
    for j, copy in enumerate(copies):
        copy.wait()
        out = jnp.dot(
            hidden_ref[...],
            down[:, j * tile : (j + 1) * tile],
            preferred_element_type=jnp.float32,
        )
        for k in range(capacity):
            for c in range(tile // LANES):
                first = k * chunks + j * (tile // LANES) + c
                stage[pl.ds(first, sources, stride=capacity * chunks), :] = out[
                    k * sources : (k + 1) * sources, c * LANES : (c + 1) * LANES
                ]
    out_ref[...] = stage[...].astype(jnp.bfloat16)


def mix_kernel(experts, capacity, routes_ref, gates_ref, back_ref, out_ref, stage):
    width = out_ref.shape[1]
    chunks = width // LANES
    block = capacity * chunks
    stage[...] = back_ref[...].astype(jnp.float32)
    picks = slot_picks(routes_ref, experts, capacity)
    gates = [jnp.sum(pick * gates_ref[...], axis=1, keepdims=True) for pick in picks]
    picks = jnp.concatenate(picks, axis=0).astype(jnp.bfloat16)
    for c in range(chunks):
        scaled = [
            (gates[k] * stage[pl.ds(k * chunks + c, experts, stride=block), :]).astype(jnp.bfloat16)
            for k in range(capacity)
        ]
        out_ref[:, c * LANES : (c + 1) * LANES] = lax.dot_general(
            picks,
            jnp.concatenate(scaled, axis=0),
            (((0,), (0,)), ((), ())),
            preferred_element_type=jnp.float32,
        ).astype(jnp.bfloat16)


def call(kernel, out_shape, scratch, flops, moved, smem=(), hbm=(), out_hbm=False):
    def spec(i):
        space = pltpu.SMEM if i in smem else pltpu.HBM if i in hbm else pltpu.VMEM
        return pl.BlockSpec(memory_space=space)

    out_space = pltpu.HBM if out_hbm else pltpu.VMEM

    def run(*args):
        args = [
            pltpu.with_memory_space_constraint(a, pltpu.HBM) if i in hbm else a
            for i, a in enumerate(args)
        ]
        return pl.pallas_call(
            kernel,
            out_shape=out_shape,
            in_specs=[spec(i) for i in range(len(args))],
            out_specs=jax.tree.map(lambda _: pl.BlockSpec(memory_space=out_space), out_shape),
            scratch_shapes=scratch,
            compiler_params=pltpu.CompilerParams(vmem_limit_bytes=VMEM_LIMIT),
            cost_estimate=pl.CostEstimate(flops=flops, bytes_accessed=moved, transcendentals=0),
        )(*args)

    return run


def on_device(latent, cotangent, routes, gates, up_weight, down_weight):
    experts = lax.axis_size("expert")
    groups = lax.axis_size("y") * lax.axis_size("core")
    tokens, width = latent.shape
    hidden_width = up_weight.shape[2]
    capacity = max(2, 3 * tokens // (2 * experts))
    slots = experts * capacity
    chunks = width // LANES
    factor = 1.0 / (tokens * groups) ** 0.5
    bf16 = functools.partial(jax.ShapeDtypeStruct, dtype=jnp.bfloat16)
    f32 = lambda *shape: pltpu.VMEM(shape, jnp.float32)
    half = lambda *shape: pltpu.VMEM(shape, jnp.bfloat16)
    route_row, gate_row = routes.reshape(1, tokens), gates.reshape(1, tokens)

    sems = lambda n: pltpu.SemaphoreType.DMA((n,))
    sent = call(
        functools.partial(pack_kernel, experts, capacity),
        bf16((2 * slots * chunks, LANES)),
        [
            f32(2 * slots * chunks, LANES),
            pltpu.VMEM((1, tokens), jnp.int32),
            f32(1, tokens),
            half(tokens, width),
            half(tokens, width),
            sems(4),
        ],
        4 * slots * tokens * width,
        4 * tokens * width + 4 * slots * width,
        hbm=(0, 1, 2, 3),
    )(route_row, gate_row, latent, cotangent)
    received = lax.all_to_all(
        sent.reshape(experts, -1, LANES), "expert", split_axis=0, concat_axis=0, tiled=True
    ).reshape(-1, LANES)
    other = lax.ppermute(received, "core", [(i, CORES - 1 - i) for i in range(CORES)])
    hidden, cots = call(
        functools.partial(hidden_kernel, experts, capacity),
        (bf16((slots, hidden_width)), bf16((slots, width))),
        [
            f32(2 * slots * chunks, LANES),
            half(slots, width),
            half(width, hidden_width),
            sems(hidden_width // (2 * LANES)),
        ],
        2 * slots * width * hidden_width,
        2 * width * hidden_width + 6 * slots * width + 2 * slots * hidden_width,
        hbm=(1,),
    )(received, up_weight[0])
    core = lax.axis_index("core").astype(jnp.int32).reshape(1)
    share = hidden_width // CORES
    partial = call(
        functools.partial(grad_kernel, experts, capacity, factor),
        bf16((share, width)),
        [
            f32(2 * slots * chunks, LANES),
            half(slots, width),
            half(CORES * slots, width),
            half(width, share),
            half(share, width),
            sems(share // LANES),
            sems(share // (2 * LANES)),
        ],
        3 * slots * width * hidden_width,
        width * hidden_width + 6 * slots * width + 2 * share * width,
        smem=(0,),
        hbm=(4,),
        out_hbm=True,
    )(core, hidden, cots, other, up_weight[0])
    down_grad = lax.psum_scatter(partial, "y", scatter_dimension=0, tiled=True)
    hidden, partial = lax.optimization_barrier((hidden, partial))
    out = call(
        functools.partial(down_kernel, experts, capacity),
        bf16((slots * chunks, LANES)),
        [
            f32(slots * chunks, LANES),
            half(hidden_width, width),
            sems(width // (2 * LANES)),
        ],
        2 * slots * width * hidden_width,
        2 * width * hidden_width + 2 * slots * width + 2 * slots * hidden_width,
        hbm=(1,),
    )(hidden, down_weight[0])
    returned = lax.all_to_all(
        out.reshape(experts, -1, LANES), "expert", split_axis=0, concat_axis=0, tiled=True
    ).reshape(-1, LANES)
    mixed = call(
        functools.partial(mix_kernel, experts, capacity),
        bf16((tokens, width)),
        [f32(slots * chunks, LANES)],
        2 * slots * tokens * width,
        2 * slots * width + 2 * tokens * width,
    )(route_row, gate_row, returned)
    return mixed, down_grad[None]


def solution(mesh):
    experts, groups = mesh.devices.shape
    split = Mesh(mesh.devices.reshape(experts, groups // CORES, CORES), ("expert", "y", "core"))
    rows = P(("expert", "y", "core"), None)
    weights = P("expert", None, None)
    return jax.shard_map(
        on_device,
        mesh=split,
        in_specs=(rows, rows, rows, rows, weights, weights),
        out_specs=(rows, P("expert", ("y", "core"), None)),
        check_vma=False,
    )
```

```python
import functools

import jax
import jax.numpy as jnp
from jax import lax
from jax.experimental import pallas as pl
from jax.experimental.pallas import tpu as pltpu
from jax.sharding import Mesh, PartitionSpec as P

LANES = 128
CORES = 2
VMEM_LIMIT = 24 * 1024 * 1024


def slot_picks(routes_ref, experts, capacity):
    tokens = routes_ref.shape[1]
    named = routes_ref[...] == lax.broadcasted_iota(jnp.int32, (experts, tokens), 0)
    earlier = lax.broadcasted_iota(jnp.int32, (tokens, tokens), 0) < lax.broadcasted_iota(
        jnp.int32, (tokens, tokens), 1
    )
    rank = jnp.dot(
        jnp.where(named, 1.0, 0.0).astype(jnp.bfloat16),
        jnp.where(earlier, 1.0, 0.0).astype(jnp.bfloat16),
        preferred_element_type=jnp.float32,
    )
    return [
        jnp.where(jnp.logical_and(named, rank == float(k)), 1.0, 0.0) for k in range(capacity)
    ]


def pack_kernel(
    experts, capacity, routes_hbm, gates_hbm, latent_hbm, cot_hbm, out_ref, stage, routes, gates, latent, cot, sems
):
    copies = [
        pltpu.make_async_copy(source, target, sems.at[i])
        for i, (source, target) in enumerate(
            ((routes_hbm, routes), (gates_hbm, gates), (latent_hbm, latent), (cot_hbm, cot))
        )
    ]
    for copy in copies:
        copy.start()
    chunks = latent.shape[1] // LANES
    block = 2 * capacity * chunks
    copies[0].wait()
    copies[1].wait()
    picks = slot_picks(routes, experts, capacity)
    for part, source in enumerate((latent, cot)):
        copies[2 + part].wait()
        for k, pick in enumerate(picks):
            rows = jnp.dot(
                pick.astype(jnp.bfloat16), source[...], preferred_element_type=jnp.float32
            )
            if part == 1:
                rows = rows * jnp.sum(pick * gates[...], axis=1, keepdims=True)
            for c in range(chunks):
                first = (2 * k + part) * chunks + c
                stage[pl.ds(first, experts, stride=block), :] = rows[:, c * LANES : (c + 1) * LANES]
    out_ref[...] = stage[...].astype(jnp.bfloat16)


def unpack(stage, out_ref, at, sources, capacity, parts, part):
    chunks = out_ref.shape[1] // LANES
    block = parts * capacity * chunks
    for k in range(capacity):
        for c in range(chunks):
            out_ref[at + k * sources : at + (k + 1) * sources, c * LANES : (c + 1) * LANES] = stage[
                pl.ds((parts * k + part) * chunks + c, sources, stride=block), :
            ].astype(jnp.bfloat16)


def activation(rows, weight):
    preact = jnp.dot(rows, weight, preferred_element_type=jnp.float32)
    return (jnp.maximum(preact, 0.0) ** 2).astype(jnp.bfloat16)


def hidden_kernel(
    sources, capacity, recv_ref, up_hbm, hidden_ref, cots_ref, up_ref, stage, rows, sems
):
    tile = 4 * LANES
    columns = [pl.ds(j * tile, tile) for j in range(up_ref.shape[1] // tile)]
    copies = [
        pltpu.make_async_copy(up_hbm.at[:, at], up_ref.at[:, at], sems.at[j])
        for j, at in enumerate(columns)
    ]
    for copy in copies:
        copy.start()
    stage[...] = recv_ref[...].astype(jnp.float32)
    unpack(stage, rows, 0, sources, capacity, 2, 0)
    unpack(stage, cots_ref, 0, sources, capacity, 2, 1)
    for copy, at in zip(copies, columns):
        copy.wait()
        hidden_ref[:, at] = activation(rows[...], up_ref[:, at])


def block_product(factor, place_ref, offset, hidden_ref, rows_ref, cots_ref, up_ref):
    y = lax.rem(place_ref[0] + offset, place_ref[2])
    at = pl.ds(pl.multiple_of((CORES * y + place_ref[1]) * LANES, LANES), LANES)
    other = activation(rows_ref[...], up_ref[:, at])
    product = lax.dot_general(
        jnp.concatenate([hidden_ref[:, at], other], axis=0),
        cots_ref[...],
        (((0,), (0,)), ((), ())),
        preferred_element_type=jnp.float32,
    )
    return (factor * product).astype(jnp.bfloat16)


def first_grad_kernel(
    sources,
    capacity,
    factor,
    offsets,
    place_ref,
    hidden_ref,
    own_cots_ref,
    other_ref,
    up_ref,
    up_block_ref,
    down_block_ref,
    rows_ref,
    cots_ref,
    stage,
):
    slots = sources * capacity
    stage[...] = other_ref[...].astype(jnp.float32)
    unpack(stage, rows_ref, 0, sources, capacity, 2, 0)
    unpack(stage, cots_ref, slots, sources, capacity, 2, 1)
    cots_ref[:slots, :] = own_cots_ref[...]
    for out_ref, offset in zip((up_block_ref, down_block_ref), offsets):
        out_ref[...] = block_product(
            factor, place_ref, offset, hidden_ref, rows_ref, cots_ref, up_ref
        )


def rest_kernel(
    sources,
    capacity,
    factor,
    offsets,
    place_ref,
    hidden_ref,
    rows_ref,
    cots_ref,
    up_ref,
    down_hbm,
    part_ref,
    out_ref,
    stage,
    down,
    sems,
):
    width = down.shape[1]
    chunks = width // LANES
    tile = 2 * LANES
    copies = [
        pltpu.make_async_copy(
            down_hbm.at[:, pl.ds(j * tile, tile)], down.at[:, pl.ds(j * tile, tile)], sems.at[j]
        )
        for j in range(width // tile)
    ]
    for copy in copies:
        copy.start()
    for i, offset in enumerate(offsets):
        part_ref[i] = block_product(
            factor, place_ref, offset, hidden_ref, rows_ref, cots_ref, up_ref
        )
    for j, copy in enumerate(copies):
        copy.wait()
        out = jnp.dot(
            hidden_ref[...],
            down[:, j * tile : (j + 1) * tile],
            preferred_element_type=jnp.float32,
        )
        for k in range(capacity):
            for c in range(tile // LANES):
                first = k * chunks + j * (tile // LANES) + c
                stage[pl.ds(first, sources, stride=capacity * chunks), :] = out[
                    k * sources : (k + 1) * sources, c * LANES : (c + 1) * LANES
                ]
    out_ref[...] = stage[...].astype(jnp.bfloat16)


def mix_kernel(experts, capacity, routes_ref, gates_ref, back_ref, out_ref, stage):
    width = out_ref.shape[1]
    chunks = width // LANES
    block = capacity * chunks
    stage[...] = back_ref[...].astype(jnp.float32)
    picks = slot_picks(routes_ref, experts, capacity)
    gates = [jnp.sum(pick * gates_ref[...], axis=1, keepdims=True) for pick in picks]
    picks = jnp.concatenate(picks, axis=0).astype(jnp.bfloat16)
    for c in range(chunks):
        scaled = [
            (gates[k] * stage[pl.ds(k * chunks + c, experts, stride=block), :]).astype(jnp.bfloat16)
            for k in range(capacity)
        ]
        out_ref[:, c * LANES : (c + 1) * LANES] = lax.dot_general(
            picks,
            jnp.concatenate(scaled, axis=0),
            (((0,), (0,)), ((), ())),
            preferred_element_type=jnp.float32,
        ).astype(jnp.bfloat16)


def call(kernel, out_shape, scratch, flops, moved, smem=(), hbm=(), out_hbm=False):
    def spec(i):
        space = pltpu.SMEM if i in smem else pltpu.HBM if i in hbm else pltpu.VMEM
        return pl.BlockSpec(memory_space=space)

    out_space = pltpu.HBM if out_hbm else pltpu.VMEM

    def run(*args):
        args = [
            pltpu.with_memory_space_constraint(a, pltpu.HBM) if i in hbm else a
            for i, a in enumerate(args)
        ]
        return pl.pallas_call(
            kernel,
            out_shape=out_shape,
            in_specs=[spec(i) for i in range(len(args))],
            out_specs=jax.tree.map(lambda _: pl.BlockSpec(memory_space=out_space), out_shape),
            scratch_shapes=scratch,
            compiler_params=pltpu.CompilerParams(vmem_limit_bytes=VMEM_LIMIT),
            cost_estimate=pl.CostEstimate(flops=flops, bytes_accessed=moved, transcendentals=0),
        )(*args)

    return run


def on_device(latent, cotangent, routes, gates, up_weight, down_weight):
    experts = lax.axis_size("expert")
    groups = lax.axis_size("y") * lax.axis_size("core")
    tokens, width = latent.shape
    hidden_width = up_weight.shape[2]
    capacity = max(2, 3 * tokens // (2 * experts))
    slots = experts * capacity
    chunks = width // LANES
    factor = 1.0 / (tokens * groups) ** 0.5
    bf16 = functools.partial(jax.ShapeDtypeStruct, dtype=jnp.bfloat16)
    f32 = lambda *shape: pltpu.VMEM(shape, jnp.float32)
    half = lambda *shape: pltpu.VMEM(shape, jnp.bfloat16)
    route_row, gate_row = routes.reshape(1, tokens), gates.reshape(1, tokens)

    sems = lambda n: pltpu.SemaphoreType.DMA((n,))
    sent = call(
        functools.partial(pack_kernel, experts, capacity),
        bf16((2 * slots * chunks, LANES)),
        [
            f32(2 * slots * chunks, LANES),
            pltpu.VMEM((1, tokens), jnp.int32),
            f32(1, tokens),
            half(tokens, width),
            half(tokens, width),
            sems(4),
        ],
        4 * slots * tokens * width,
        4 * tokens * width + 4 * slots * width,
        hbm=(0, 1, 2, 3),
    )(route_row, gate_row, latent, cotangent)
    received = lax.all_to_all(
        sent.reshape(experts, -1, LANES), "expert", split_axis=0, concat_axis=0, tiled=True
    ).reshape(-1, LANES)
    other = lax.ppermute(received, "core", [(i, CORES - 1 - i) for i in range(CORES)])
    hidden, cots, up = call(
        functools.partial(hidden_kernel, experts, capacity),
        (
            bf16((slots, hidden_width)),
            bf16((slots, width)),
            bf16((width, hidden_width)),
        ),
        [
            f32(2 * slots * chunks, LANES),
            half(slots, width),
            sems(hidden_width // (4 * LANES)),
        ],
        2 * slots * width * hidden_width,
        2 * width * hidden_width + 6 * slots * width + 2 * slots * hidden_width,
        hbm=(1,),
    )(received, up_weight[0])
    ring = lax.axis_size("y")
    far, near = ring // 2, (ring - 1) // 2
    place = jnp.stack([lax.axis_index("y"), lax.axis_index("core"), ring]).astype(jnp.int32)
    block = (hidden_width // (ring * CORES), width)
    firsts = (far, ring - near)
    rest = tuple(i for i in range(ring) if i not in firsts)
    upward, downward, rows, cots = call(
        functools.partial(first_grad_kernel, experts, capacity, factor, firsts),
        (bf16(block), bf16(block), bf16((slots, width)), bf16((CORES * slots, width))),
        [f32(2 * slots * chunks, LANES)],
        3 * slots * width * hidden_width * 2 // ring,
        8 * slots * width,
        smem=(0,),
    )(place, hidden, cots, other, up)
    parts, out = call(
        functools.partial(rest_kernel, experts, capacity, factor, rest),
        (bf16((len(rest),) + block), bf16((slots * chunks, LANES))),
        [
            f32(slots * chunks, LANES),
            half(hidden_width, width),
            sems(width // (2 * LANES)),
        ],
        5 * slots * width * hidden_width,
        2 * width * hidden_width + 8 * slots * width,
        smem=(0,),
        hbm=(5,),
    )(place, hidden, rows, cots, up, down_weight[0])
    after = [(i, (i + 1) % ring) for i in range(ring)]
    before = [(i, (i - 1) % ring) for i in range(ring)]

    def add(*terms):
        return sum(term.astype(jnp.float32) for term in terms)

    total = parts[rest.index(0)]
    for hop in range(far):
        upward = lax.ppermute(upward, "y", after)
        if hop < near:
            downward = lax.ppermute(downward, "y", before)
        if hop < far - 1:
            upward = add(upward, parts[rest.index(far - 1 - hop)]).astype(jnp.bfloat16)
        if hop < near - 1:
            downward = add(downward, parts[rest.index(ring - near + 1 + hop)]).astype(jnp.bfloat16)
    down_grad = add(total, upward, downward).astype(jnp.bfloat16)
    returned = lax.all_to_all(
        out.reshape(experts, -1, LANES), "expert", split_axis=0, concat_axis=0, tiled=True
    ).reshape(-1, LANES)
    mixed = call(
        functools.partial(mix_kernel, experts, capacity),
        bf16((tokens, width)),
        [f32(slots * chunks, LANES)],
        2 * slots * tokens * width,
        2 * slots * width + 2 * tokens * width,
    )(route_row, gate_row, returned)
    return mixed, down_grad[None]


def solution(mesh):
    experts, groups = mesh.devices.shape
    split = Mesh(mesh.devices.reshape(experts, groups // CORES, CORES), ("expert", "y", "core"))
    rows = P(("expert", "y", "core"), None)
    weights = P("expert", None, None)
    return jax.shard_map(
        on_device,
        mesh=split,
        in_specs=(rows, rows, rows, rows, weights, weights),
        out_specs=(rows, P("expert", ("y", "core"), None)),
        check_vma=False,
    )
```

```python
import functools

import jax
import jax.numpy as jnp
from jax import lax
from jax.experimental import pallas as pl
from jax.experimental.pallas import tpu as pltpu
from jax.sharding import Mesh, PartitionSpec as P

LANES = 128
ADD_WEIGHT = 20000
CORES = 2
VMEM_LIMIT = 24 * 1024 * 1024


def slot_picks(routes_ref, experts, capacity):
    tokens = routes_ref.shape[1]
    named = routes_ref[...] == lax.broadcasted_iota(jnp.int32, (experts, tokens), 0)
    earlier = lax.broadcasted_iota(jnp.int32, (tokens, tokens), 0) < lax.broadcasted_iota(
        jnp.int32, (tokens, tokens), 1
    )
    rank = jnp.dot(
        jnp.where(named, 1.0, 0.0).astype(jnp.bfloat16),
        jnp.where(earlier, 1.0, 0.0).astype(jnp.bfloat16),
        preferred_element_type=jnp.float32,
    )
    return [
        jnp.where(jnp.logical_and(named, rank == float(k)), 1.0, 0.0) for k in range(capacity)
    ]


def pack_kernel(
    experts, capacity, routes_hbm, gates_hbm, latent_hbm, cot_hbm, out_ref, stage, routes, gates, latent, cot, sems
):
    copies = [
        pltpu.make_async_copy(source, target, sems.at[i])
        for i, (source, target) in enumerate(
            ((routes_hbm, routes), (gates_hbm, gates), (latent_hbm, latent), (cot_hbm, cot))
        )
    ]
    for copy in copies:
        copy.start()
    chunks = latent.shape[1] // LANES
    block = 2 * capacity * chunks
    copies[0].wait()
    copies[1].wait()
    picks = slot_picks(routes, experts, capacity)
    for part, source in enumerate((latent, cot)):
        copies[2 + part].wait()
        for k, pick in enumerate(picks):
            rows = jnp.dot(
                pick.astype(jnp.bfloat16), source[...], preferred_element_type=jnp.float32
            )
            if part == 1:
                rows = rows * jnp.sum(pick * gates[...], axis=1, keepdims=True)
            for c in range(chunks):
                first = (2 * k + part) * chunks + c
                stage[pl.ds(first, experts, stride=block), :] = rows[:, c * LANES : (c + 1) * LANES]
    out_ref[...] = stage[...].astype(jnp.bfloat16)


def unpack(stage, out_ref, at, sources, capacity, parts, part):
    chunks = out_ref.shape[1] // LANES
    block = parts * capacity * chunks
    for k in range(capacity):
        for c in range(chunks):
            out_ref[at + k * sources : at + (k + 1) * sources, c * LANES : (c + 1) * LANES] = stage[
                pl.ds((parts * k + part) * chunks + c, sources, stride=block), :
            ].astype(jnp.bfloat16)


def activation(rows, weight):
    preact = jnp.dot(rows, weight, preferred_element_type=jnp.float32)
    return (jnp.maximum(preact, 0.0) ** 2).astype(jnp.bfloat16)


def hidden_kernel(
    sources, capacity, recv_ref, up_hbm, hidden_ref, cots_ref, up_ref, stage, rows, sems
):
    tile = 4 * LANES
    columns = [pl.ds(j * tile, tile) for j in range(up_ref.shape[1] // tile)]
    copies = [
        pltpu.make_async_copy(up_hbm.at[:, at], up_ref.at[:, at], sems.at[j])
        for j, at in enumerate(columns)
    ]
    for copy in copies:
        copy.start()
    stage[...] = recv_ref[...].astype(jnp.float32)
    unpack(stage, rows, 0, sources, capacity, 2, 0)
    unpack(stage, cots_ref, 0, sources, capacity, 2, 1)
    for copy, at in zip(copies, columns):
        copy.wait()
        hidden_ref[:, at] = activation(rows[...], up_ref[:, at])


def block_products(factor, place_ref, offsets, hidden_ref, rows_ref, cots_ref, up_ref):
    columns = []
    for offset in offsets:
        y = lax.rem(place_ref[0] + offset, place_ref[2])
        columns.append(pl.ds(pl.multiple_of((CORES * y + place_ref[1]) * LANES, LANES), LANES))

    def gather(ref):
        return jnp.concatenate([ref[:, at] for at in columns], axis=1)

    product = lax.dot_general(
        jnp.concatenate([gather(hidden_ref), activation(rows_ref[...], gather(up_ref))], axis=0),
        cots_ref[...],
        (((0,), (0,)), ((), ())),
        preferred_element_type=jnp.float32,
    )
    product = (factor * product).astype(jnp.bfloat16)
    return [product[i * LANES : (i + 1) * LANES] for i in range(len(offsets))]


def first_grad_kernel(
    sources,
    capacity,
    factor,
    offsets,
    place_ref,
    hidden_ref,
    own_cots_ref,
    other_ref,
    up_ref,
    up_block_ref,
    down_block_ref,
    rows_ref,
    cots_ref,
    stage,
):
    slots = sources * capacity
    stage[...] = other_ref[...].astype(jnp.float32)
    unpack(stage, rows_ref, 0, sources, capacity, 2, 0)
    unpack(stage, cots_ref, slots, sources, capacity, 2, 1)
    cots_ref[:slots, :] = own_cots_ref[...]
    up_block_ref[...], down_block_ref[...] = block_products(
        factor, place_ref, offsets, hidden_ref, rows_ref, cots_ref, up_ref
    )


def rest_kernel(
    sources,
    capacity,
    factor,
    offsets,
    place_ref,
    hidden_ref,
    rows_ref,
    cots_ref,
    up_ref,
    down_hbm,
    part_ref,
    out_ref,
    stage,
    down,
    sems,
):
    width = down.shape[1]
    chunks = width // LANES
    tile = 2 * LANES
    copies = [
        pltpu.make_async_copy(
            down_hbm.at[:, pl.ds(j * tile, tile)], down.at[:, pl.ds(j * tile, tile)], sems.at[j]
        )
        for j in range(width // tile)
    ]
    for copy in copies:
        copy.start()
    for i in range(0, len(offsets), 2):
        pair = offsets[i : i + 2]
        for j, product in enumerate(
            block_products(factor, place_ref, pair, hidden_ref, rows_ref, cots_ref, up_ref)
        ):
            part_ref[i + j] = product
    for j, copy in enumerate(copies):
        copy.wait()
        out = jnp.dot(
            hidden_ref[...],
            down[:, j * tile : (j + 1) * tile],
            preferred_element_type=jnp.float32,
        )
        for k in range(capacity):
            for c in range(tile // LANES):
                first = k * chunks + j * (tile // LANES) + c
                stage[pl.ds(first, sources, stride=capacity * chunks), :] = out[
                    k * sources : (k + 1) * sources, c * LANES : (c + 1) * LANES
                ]
    out_ref[...] = stage[...].astype(jnp.bfloat16)


def add_kernel(index, arrived_ref, part_ref, out_ref):
    out_ref[...] = (
        arrived_ref[...].astype(jnp.float32) + part_ref[index].astype(jnp.float32)
    ).astype(jnp.bfloat16)


def mix_kernel(experts, capacity, routes_ref, gates_ref, back_ref, out_ref, stage):
    width = out_ref.shape[1]
    chunks = width // LANES
    block = capacity * chunks
    stage[...] = back_ref[...].astype(jnp.float32)
    picks = slot_picks(routes_ref, experts, capacity)
    gates = [jnp.sum(pick * gates_ref[...], axis=1, keepdims=True) for pick in picks]
    picks = jnp.concatenate(picks, axis=0).astype(jnp.bfloat16)
    for c in range(chunks):
        scaled = [
            (gates[k] * stage[pl.ds(k * chunks + c, experts, stride=block), :]).astype(jnp.bfloat16)
            for k in range(capacity)
        ]
        out_ref[:, c * LANES : (c + 1) * LANES] = lax.dot_general(
            picks,
            jnp.concatenate(scaled, axis=0),
            (((0,), (0,)), ((), ())),
            preferred_element_type=jnp.float32,
        ).astype(jnp.bfloat16)


def call(kernel, out_shape, scratch, flops, moved, smem=(), hbm=(), out_hbm=False):
    def spec(i):
        space = pltpu.SMEM if i in smem else pltpu.HBM if i in hbm else pltpu.VMEM
        return pl.BlockSpec(memory_space=space)

    out_space = pltpu.HBM if out_hbm else pltpu.VMEM

    def run(*args):
        args = [
            pltpu.with_memory_space_constraint(a, pltpu.HBM) if i in hbm else a
            for i, a in enumerate(args)
        ]
        return pl.pallas_call(
            kernel,
            out_shape=out_shape,
            in_specs=[spec(i) for i in range(len(args))],
            out_specs=jax.tree.map(lambda _: pl.BlockSpec(memory_space=out_space), out_shape),
            scratch_shapes=scratch,
            compiler_params=pltpu.CompilerParams(vmem_limit_bytes=VMEM_LIMIT),
            cost_estimate=pl.CostEstimate(flops=flops, bytes_accessed=moved, transcendentals=0),
        )(*args)

    return run


def on_device(latent, cotangent, routes, gates, up_weight, down_weight):
    experts = lax.axis_size("expert")
    groups = lax.axis_size("y") * lax.axis_size("core")
    tokens, width = latent.shape
    hidden_width = up_weight.shape[2]
    capacity = max(2, 3 * tokens // (2 * experts))
    slots = experts * capacity
    chunks = width // LANES
    factor = 1.0 / (tokens * groups) ** 0.5
    bf16 = functools.partial(jax.ShapeDtypeStruct, dtype=jnp.bfloat16)
    f32 = lambda *shape: pltpu.VMEM(shape, jnp.float32)
    half = lambda *shape: pltpu.VMEM(shape, jnp.bfloat16)
    route_row, gate_row = routes.reshape(1, tokens), gates.reshape(1, tokens)

    sems = lambda n: pltpu.SemaphoreType.DMA((n,))
    sent = call(
        functools.partial(pack_kernel, experts, capacity),
        bf16((2 * slots * chunks, LANES)),
        [
            f32(2 * slots * chunks, LANES),
            pltpu.VMEM((1, tokens), jnp.int32),
            f32(1, tokens),
            half(tokens, width),
            half(tokens, width),
            sems(4),
        ],
        4 * slots * tokens * width,
        4 * tokens * width + 4 * slots * width,
        hbm=(0, 1, 2, 3),
    )(route_row, gate_row, latent, cotangent)
    received = lax.all_to_all(
        sent.reshape(experts, -1, LANES), "expert", split_axis=0, concat_axis=0, tiled=True
    ).reshape(-1, LANES)
    other = lax.ppermute(received, "core", [(i, CORES - 1 - i) for i in range(CORES)])
    hidden, cots, up = call(
        functools.partial(hidden_kernel, experts, capacity),
        (
            bf16((slots, hidden_width)),
            bf16((slots, width)),
            bf16((width, hidden_width)),
        ),
        [
            f32(2 * slots * chunks, LANES),
            half(slots, width),
            sems(hidden_width // (4 * LANES)),
        ],
        2 * slots * width * hidden_width,
        2 * width * hidden_width + 6 * slots * width + 2 * slots * hidden_width,
        hbm=(1,),
    )(received, up_weight[0])
    ring = lax.axis_size("y")
    far, near = ring // 2, (ring - 1) // 2
    place = jnp.stack([lax.axis_index("y"), lax.axis_index("core"), ring]).astype(jnp.int32)
    block = (hidden_width // (ring * CORES), width)
    firsts = (far, ring - near)
    rest = tuple(i for i in range(ring) if i not in firsts)
    upward, downward, rows, cots = call(
        functools.partial(first_grad_kernel, experts, capacity, factor, firsts),
        (bf16(block), bf16(block), bf16((slots, width)), bf16((CORES * slots, width))),
        [f32(2 * slots * chunks, LANES)],
        3 * slots * width * hidden_width * 2 // ring,
        8 * slots * width,
        smem=(0,),
    )(place, hidden, cots, other, up)
    parts, out = call(
        functools.partial(rest_kernel, experts, capacity, factor, rest),
        (bf16((len(rest),) + block), bf16((slots * chunks, LANES))),
        [
            f32(slots * chunks, LANES),
            half(hidden_width, width),
            sems(width // (2 * LANES)),
        ],
        5 * slots * width * hidden_width,
        2 * width * hidden_width + 8 * slots * width,
        smem=(0,),
        hbm=(5,),
    )(place, hidden, rows, cots, up, down_weight[0])
    after = [(i, (i + 1) % ring) for i in range(ring)]
    before = [(i, (i - 1) % ring) for i in range(ring)]

    def add(arrived, offset):
        return call(
            functools.partial(add_kernel, rest.index(offset)),
            bf16(block),
            [],
            ADD_WEIGHT * block[0] * block[1],
            6 * block[0] * block[1],
        )(arrived, parts)

    total = parts[rest.index(0)]
    for hop in range(far):
        upward = lax.ppermute(upward, "y", after)
        if hop < near:
            downward = lax.ppermute(downward, "y", before)
        if hop < far - 1:
            upward = add(upward, far - 1 - hop)
        if hop < near - 1:
            downward = add(downward, ring - near + 1 + hop)
    returned = lax.all_to_all(
        out.reshape(experts, -1, LANES), "expert", split_axis=0, concat_axis=0, tiled=True
    ).reshape(-1, LANES)
    mixed = call(
        functools.partial(mix_kernel, experts, capacity),
        bf16((tokens, width)),
        [f32(slots * chunks, LANES)],
        2 * slots * tokens * width,
        2 * slots * width + 2 * tokens * width,
    )(route_row, gate_row, returned)
    mixed, upward, downward = lax.optimization_barrier((mixed, upward, downward))
    down_grad = sum(term.astype(jnp.float32) for term in (total, upward, downward)).astype(
        jnp.bfloat16
    )
    return mixed, down_grad[None]


def solution(mesh):
    experts, groups = mesh.devices.shape
    split = Mesh(mesh.devices.reshape(experts, groups // CORES, CORES), ("expert", "y", "core"))
    rows = P(("expert", "y", "core"), None)
    weights = P("expert", None, None)
    return jax.shard_map(
        on_device,
        mesh=split,
        in_specs=(rows, rows, rows, rows, weights, weights),
        out_specs=(rows, P("expert", ("y", "core"), None)),
        check_vma=False,
    )
```

```python
import functools

import jax
import jax.numpy as jnp
from jax import lax
from jax.experimental import pallas as pl
from jax.experimental.pallas import tpu as pltpu
from jax.sharding import Mesh, PartitionSpec as P

LANES = 128
ADD_WEIGHT = 20000
CORES = 2
VMEM_LIMIT = 24 * 1024 * 1024


def slot_picks(routes_ref, experts, capacity):
    tokens = routes_ref.shape[1]
    named = routes_ref[...] == lax.broadcasted_iota(jnp.int32, (experts, tokens), 0)
    earlier = lax.broadcasted_iota(jnp.int32, (tokens, tokens), 0) < lax.broadcasted_iota(
        jnp.int32, (tokens, tokens), 1
    )
    rank = jnp.dot(
        jnp.where(named, 1.0, 0.0).astype(jnp.bfloat16),
        jnp.where(earlier, 1.0, 0.0).astype(jnp.bfloat16),
        preferred_element_type=jnp.float32,
    )
    return [
        jnp.where(jnp.logical_and(named, rank == float(k)), 1.0, 0.0) for k in range(capacity)
    ]


def pack_kernel(
    experts, capacity, routes_hbm, gates_hbm, latent_hbm, cot_hbm, out_ref, stage, routes, gates, latent, cot, sems
):
    copies = [
        pltpu.make_async_copy(source, target, sems.at[i])
        for i, (source, target) in enumerate(
            ((routes_hbm, routes), (gates_hbm, gates), (latent_hbm, latent), (cot_hbm, cot))
        )
    ]
    for copy in copies:
        copy.start()
    chunks = latent.shape[1] // LANES
    block = 2 * capacity * chunks
    copies[0].wait()
    copies[1].wait()
    picks = slot_picks(routes, experts, capacity)
    for part, source in enumerate((latent, cot)):
        copies[2 + part].wait()
        for k, pick in enumerate(picks):
            rows = jnp.dot(
                pick.astype(jnp.bfloat16), source[...], preferred_element_type=jnp.float32
            )
            if part == 1:
                rows = rows * jnp.sum(pick * gates[...], axis=1, keepdims=True)
            for c in range(chunks):
                first = (2 * k + part) * chunks + c
                stage[pl.ds(first, experts, stride=block), :] = rows[:, c * LANES : (c + 1) * LANES]
    out_ref[...] = stage[...].astype(jnp.bfloat16)


def unpack(stage, out_ref, at, sources, capacity, parts, part):
    chunks = out_ref.shape[1] // LANES
    block = parts * capacity * chunks
    for k in range(capacity):
        for c in range(chunks):
            out_ref[at + k * sources : at + (k + 1) * sources, c * LANES : (c + 1) * LANES] = stage[
                pl.ds((parts * k + part) * chunks + c, sources, stride=block), :
            ].astype(jnp.bfloat16)


def activation(rows, weight):
    preact = jnp.dot(rows, weight, preferred_element_type=jnp.float32)
    return (jnp.maximum(preact, 0.0) ** 2).astype(jnp.bfloat16)


def hidden_kernel(
    sources, capacity, recv_ref, up_hbm, hidden_ref, cots_ref, up_ref, stage, rows, sems
):
    tile = 4 * LANES
    columns = [pl.ds(j * tile, tile) for j in range(up_ref.shape[1] // tile)]
    copies = [
        pltpu.make_async_copy(up_hbm.at[:, at], up_ref.at[:, at], sems.at[j])
        for j, at in enumerate(columns)
    ]
    for copy in copies:
        copy.start()
    stage[...] = recv_ref[...].astype(jnp.float32)
    unpack(stage, rows, 0, sources, capacity, 2, 0)
    unpack(stage, cots_ref, 0, sources, capacity, 2, 1)
    for copy, at in zip(copies, columns):
        copy.wait()
        hidden_ref[:, at] = activation(rows[...], up_ref[:, at])


def grad_kernel(
    sources,
    capacity,
    factor,
    offsets,
    place_ref,
    hidden_ref,
    own_cots_ref,
    other_ref,
    up_ref,
    down_hbm,
    up_block_ref,
    down_block_ref,
    part_ref,
    down_ref,
    stage,
    rows,
    cots,
    acts,
    sem,
):
    fetch = pltpu.make_async_copy(down_hbm, down_ref, sem)
    fetch.start()
    slots = sources * capacity
    stage[...] = other_ref[...].astype(jnp.float32)
    unpack(stage, rows, 0, sources, capacity, 2, 0)
    unpack(stage, cots, slots, sources, capacity, 2, 1)
    cots[:slots, :] = own_cots_ref[...]
    for j in range(0, len(offsets), 4):
        columns = []
        for offset in offsets[j : j + 4]:
            y = lax.rem(place_ref[0] + offset, place_ref[2])
            columns.append(pl.ds(pl.multiple_of((CORES * y + place_ref[1]) * LANES, LANES), LANES))
        at = pl.ds(j * LANES, 4 * LANES)
        weight = jnp.concatenate([up_ref[:, column] for column in columns], axis=1)
        acts[:slots, at] = jnp.concatenate([hidden_ref[:, column] for column in columns], axis=1)
        acts[slots:, at] = activation(rows[...], weight)
    product = lax.dot_general(
        acts[...], cots[...], (((0,), (0,)), ((), ())), preferred_element_type=jnp.float32
    )
    product = (factor * product).astype(jnp.bfloat16)
    up_block_ref[...] = product[:LANES]
    down_block_ref[...] = product[LANES : 2 * LANES]
    for j in range(len(offsets) - 2):
        part_ref[j] = product[(j + 2) * LANES : (j + 3) * LANES]
    fetch.wait()


def down_kernel(sources, capacity, hidden_ref, down_ref, out_ref, stage):
    width = down_ref.shape[1]
    chunks = width // LANES
    out = jnp.dot(hidden_ref[...], down_ref[...], preferred_element_type=jnp.float32)
    for k in range(capacity):
        for c in range(chunks):
            stage[pl.ds(k * chunks + c, sources, stride=capacity * chunks), :] = out[
                k * sources : (k + 1) * sources, c * LANES : (c + 1) * LANES
            ]
    out_ref[...] = stage[...].astype(jnp.bfloat16)


def add_kernel(index, arrived_ref, part_ref, out_ref):
    out_ref[...] = (
        arrived_ref[...].astype(jnp.float32) + part_ref[index].astype(jnp.float32)
    ).astype(jnp.bfloat16)


def mix_kernel(experts, capacity, routes_ref, gates_ref, back_ref, out_ref, stage):
    width = out_ref.shape[1]
    chunks = width // LANES
    block = capacity * chunks
    stage[...] = back_ref[...].astype(jnp.float32)
    picks = slot_picks(routes_ref, experts, capacity)
    gates = [jnp.sum(pick * gates_ref[...], axis=1, keepdims=True) for pick in picks]
    picks = jnp.concatenate(picks, axis=0).astype(jnp.bfloat16)
    for c in range(chunks):
        scaled = [
            (gates[k] * stage[pl.ds(k * chunks + c, experts, stride=block), :]).astype(jnp.bfloat16)
            for k in range(capacity)
        ]
        out_ref[:, c * LANES : (c + 1) * LANES] = lax.dot_general(
            picks,
            jnp.concatenate(scaled, axis=0),
            (((0,), (0,)), ((), ())),
            preferred_element_type=jnp.float32,
        ).astype(jnp.bfloat16)


def call(kernel, out_shape, scratch, flops, moved, smem=(), hbm=(), out_hbm=False):
    def spec(i):
        space = pltpu.SMEM if i in smem else pltpu.HBM if i in hbm else pltpu.VMEM
        return pl.BlockSpec(memory_space=space)

    out_space = pltpu.HBM if out_hbm else pltpu.VMEM

    def run(*args):
        args = [
            pltpu.with_memory_space_constraint(a, pltpu.HBM) if i in hbm else a
            for i, a in enumerate(args)
        ]
        return pl.pallas_call(
            kernel,
            out_shape=out_shape,
            in_specs=[spec(i) for i in range(len(args))],
            out_specs=jax.tree.map(lambda _: pl.BlockSpec(memory_space=out_space), out_shape),
            scratch_shapes=scratch,
            compiler_params=pltpu.CompilerParams(vmem_limit_bytes=VMEM_LIMIT),
            cost_estimate=pl.CostEstimate(flops=flops, bytes_accessed=moved, transcendentals=0),
        )(*args)

    return run


def on_device(latent, cotangent, routes, gates, up_weight, down_weight):
    experts = lax.axis_size("expert")
    groups = lax.axis_size("y") * lax.axis_size("core")
    tokens, width = latent.shape
    hidden_width = up_weight.shape[2]
    capacity = max(2, 3 * tokens // (2 * experts))
    slots = experts * capacity
    chunks = width // LANES
    factor = 1.0 / (tokens * groups) ** 0.5
    bf16 = functools.partial(jax.ShapeDtypeStruct, dtype=jnp.bfloat16)
    f32 = lambda *shape: pltpu.VMEM(shape, jnp.float32)
    half = lambda *shape: pltpu.VMEM(shape, jnp.bfloat16)
    route_row, gate_row = routes.reshape(1, tokens), gates.reshape(1, tokens)

    sems = lambda n: pltpu.SemaphoreType.DMA((n,))
    sent = call(
        functools.partial(pack_kernel, experts, capacity),
        bf16((2 * slots * chunks, LANES)),
        [
            f32(2 * slots * chunks, LANES),
            pltpu.VMEM((1, tokens), jnp.int32),
            f32(1, tokens),
            half(tokens, width),
            half(tokens, width),
            sems(4),
        ],
        4 * slots * tokens * width,
        4 * tokens * width + 4 * slots * width,
        hbm=(0, 1, 2, 3),
    )(route_row, gate_row, latent, cotangent)
    received = lax.all_to_all(
        sent.reshape(experts, -1, LANES), "expert", split_axis=0, concat_axis=0, tiled=True
    ).reshape(-1, LANES)
    other = lax.ppermute(received, "core", [(i, CORES - 1 - i) for i in range(CORES)])
    hidden, cots, up = call(
        functools.partial(hidden_kernel, experts, capacity),
        (
            bf16((slots, hidden_width)),
            bf16((slots, width)),
            bf16((width, hidden_width)),
        ),
        [
            f32(2 * slots * chunks, LANES),
            half(slots, width),
            sems(hidden_width // (4 * LANES)),
        ],
        2 * slots * width * hidden_width,
        2 * width * hidden_width + 6 * slots * width + 2 * slots * hidden_width,
        hbm=(1,),
    )(received, up_weight[0])
    ring = lax.axis_size("y")
    far, near = ring // 2, (ring - 1) // 2
    place = jnp.stack([lax.axis_index("y"), lax.axis_index("core"), ring]).astype(jnp.int32)
    block = (hidden_width // (ring * CORES), width)
    firsts = (far, ring - near)
    rest = tuple(i for i in range(ring) if i not in firsts)
    upward, downward, parts, down = call(
        functools.partial(grad_kernel, experts, capacity, factor, firsts + rest),
        (
            bf16(block),
            bf16(block),
            bf16((len(rest),) + block),
            bf16((hidden_width, width)),
        ),
        [
            f32(2 * slots * chunks, LANES),
            half(slots, width),
            half(CORES * slots, width),
            half(CORES * slots, hidden_width // CORES),
            pltpu.SemaphoreType.DMA,
        ],
        3 * slots * width * hidden_width,
        2 * width * hidden_width + 8 * slots * width,
        smem=(0,),
        hbm=(5,),
    )(place, hidden, cots, other, up, down_weight[0])
    out = call(
        functools.partial(down_kernel, experts, capacity),
        bf16((slots * chunks, LANES)),
        [f32(slots * chunks, LANES)],
        2 * slots * width * hidden_width,
        2 * width * hidden_width + 4 * slots * width,
    )(hidden, down)
    after = [(i, (i + 1) % ring) for i in range(ring)]
    before = [(i, (i - 1) % ring) for i in range(ring)]

    def add(arrived, offset):
        return call(
            functools.partial(add_kernel, rest.index(offset)),
            bf16(block),
            [],
            ADD_WEIGHT * block[0] * block[1],
            6 * block[0] * block[1],
        )(arrived, parts)

    total = parts[rest.index(0)]
    for hop in range(far):
        upward = lax.ppermute(upward, "y", after)
        if hop == 0:
            upward, downward = lax.optimization_barrier((upward, downward))
        if hop < far - 1:
            upward = add(upward, far - 1 - hop)
    for hop in range(near):
        downward = lax.ppermute(downward, "y", before)
        if hop < near - 1:
            downward = add(downward, ring - near + 1 + hop)
    returned = lax.all_to_all(
        out.reshape(experts, -1, LANES), "expert", split_axis=0, concat_axis=0, tiled=True
    ).reshape(-1, LANES)
    mixed = call(
        functools.partial(mix_kernel, experts, capacity),
        bf16((tokens, width)),
        [f32(slots * chunks, LANES)],
        2 * slots * tokens * width,
        2 * slots * width + 2 * tokens * width,
    )(route_row, gate_row, returned)
    mixed, upward, downward = lax.optimization_barrier((mixed, upward, downward))
    down_grad = sum(term.astype(jnp.float32) for term in (total, upward, downward)).astype(
        jnp.bfloat16
    )
    return mixed, down_grad[None]


def solution(mesh):
    experts, groups = mesh.devices.shape
    split = Mesh(mesh.devices.reshape(experts, groups // CORES, CORES), ("expert", "y", "core"))
    rows = P(("expert", "y", "core"), None)
    weights = P("expert", None, None)
    return jax.shard_map(
        on_device,
        mesh=split,
        in_specs=(rows, rows, rows, rows, weights, weights),
        out_specs=(rows, P("expert", ("y", "core"), None)),
        check_vma=False,
    )
```

```python
import functools

import jax
import jax.numpy as jnp
from jax import lax
from jax.experimental import pallas as pl
from jax.experimental.pallas import tpu as pltpu
from jax.sharding import Mesh, PartitionSpec as P

LANES = 128
ADD_WEIGHT = 20000
CORES = 2
VMEM_LIMIT = 24 * 1024 * 1024


def slot_picks(routes_ref, experts, capacity):
    tokens = routes_ref.shape[1]
    named = routes_ref[...] == lax.broadcasted_iota(jnp.int32, (experts, tokens), 0)
    earlier = lax.broadcasted_iota(jnp.int32, (tokens, tokens), 0) < lax.broadcasted_iota(
        jnp.int32, (tokens, tokens), 1
    )
    rank = jnp.dot(
        jnp.where(named, 1.0, 0.0).astype(jnp.bfloat16),
        jnp.where(earlier, 1.0, 0.0).astype(jnp.bfloat16),
        preferred_element_type=jnp.float32,
    )
    return [
        jnp.where(jnp.logical_and(named, rank == float(k)), 1.0, 0.0) for k in range(capacity)
    ]


def pack_kernel(
    experts, capacity, routes_hbm, gates_hbm, latent_hbm, cot_hbm, out_ref, stage, routes, gates, latent, cot, sems
):
    copies = [
        pltpu.make_async_copy(source, target, sems.at[i])
        for i, (source, target) in enumerate(
            ((routes_hbm, routes), (gates_hbm, gates), (latent_hbm, latent), (cot_hbm, cot))
        )
    ]
    for copy in copies:
        copy.start()
    chunks = latent.shape[1] // LANES
    block = 2 * capacity * chunks
    copies[0].wait()
    copies[1].wait()
    picks = slot_picks(routes, experts, capacity)
    for part, source in enumerate((latent, cot)):
        copies[2 + part].wait()
        for k, pick in enumerate(picks):
            rows = jnp.dot(
                pick.astype(jnp.bfloat16), source[...], preferred_element_type=jnp.float32
            )
            if part == 1:
                rows = rows * jnp.sum(pick * gates[...], axis=1, keepdims=True)
            for c in range(chunks):
                first = (2 * k + part) * chunks + c
                stage[pl.ds(first, experts, stride=block), :] = rows[:, c * LANES : (c + 1) * LANES]
    out_ref[...] = stage[...].astype(jnp.bfloat16)


def unpack(stage, out_ref, at, sources, capacity, parts, part):
    chunks = out_ref.shape[1] // LANES
    block = parts * capacity * chunks
    for k in range(capacity):
        for c in range(chunks):
            out_ref[at + k * sources : at + (k + 1) * sources, c * LANES : (c + 1) * LANES] = stage[
                pl.ds((parts * k + part) * chunks + c, sources, stride=block), :
            ].astype(jnp.bfloat16)


def activation(rows, weight):
    preact = jnp.dot(rows, weight, preferred_element_type=jnp.float32)
    return (jnp.maximum(preact, 0.0) ** 2).astype(jnp.bfloat16)


def hidden_kernel(
    sources, capacity, recv_ref, up_hbm, hidden_ref, cots_ref, up_ref, stage, rows, sems
):
    tile = 4 * LANES
    columns = [pl.ds(j * tile, tile) for j in range(up_ref.shape[1] // tile)]
    copies = [
        pltpu.make_async_copy(up_hbm.at[:, at], up_ref.at[:, at], sems.at[j])
        for j, at in enumerate(columns)
    ]
    for copy in copies:
        copy.start()
    stage[...] = recv_ref[...].astype(jnp.float32)
    unpack(stage, rows, 0, sources, capacity, 2, 0)
    unpack(stage, cots_ref, 0, sources, capacity, 2, 1)
    for copy, at in zip(copies, columns):
        copy.wait()
        hidden_ref[:, at] = activation(rows[...], up_ref[:, at])


def grad_kernel(
    sources,
    capacity,
    factor,
    offsets,
    place_ref,
    hidden_ref,
    own_cots_ref,
    other_ref,
    up_ref,
    down_hbm,
    up_block_ref,
    down_block_ref,
    part_ref,
    down_ref,
    stage,
    rows,
    cots,
    acts,
    sem,
):
    fetch = pltpu.make_async_copy(down_hbm, down_ref, sem)
    fetch.start()
    slots = sources * capacity
    stage[...] = other_ref[...].astype(jnp.float32)
    unpack(stage, rows, 0, sources, capacity, 2, 0)
    unpack(stage, cots, slots, sources, capacity, 2, 1)
    cots[:slots, :] = own_cots_ref[...]
    for j in range(0, len(offsets), 4):
        columns = []
        for offset in offsets[j : j + 4]:
            turn = jnp.where(place_ref[1] == 0, offset, place_ref[2] - offset)
            y = lax.rem(place_ref[0] + turn, place_ref[2])
            columns.append(pl.ds(pl.multiple_of((CORES * y + place_ref[1]) * LANES, LANES), LANES))
        at = pl.ds(j * LANES, 4 * LANES)
        weight = jnp.concatenate([up_ref[:, column] for column in columns], axis=1)
        acts[:slots, at] = jnp.concatenate([hidden_ref[:, column] for column in columns], axis=1)
        acts[slots:, at] = activation(rows[...], weight)
    product = lax.dot_general(
        acts[...], cots[...], (((0,), (0,)), ((), ())), preferred_element_type=jnp.float32
    )
    product = (factor * product).astype(jnp.bfloat16)
    up_block_ref[...] = product[:LANES]
    down_block_ref[...] = product[LANES : 2 * LANES]
    for j in range(len(offsets) - 2):
        part_ref[j] = product[(j + 2) * LANES : (j + 3) * LANES]
    fetch.wait()


def down_kernel(sources, capacity, hidden_ref, down_ref, out_ref, stage):
    width = down_ref.shape[1]
    chunks = width // LANES
    out = jnp.dot(hidden_ref[...], down_ref[...], preferred_element_type=jnp.float32)
    for k in range(capacity):
        for c in range(chunks):
            stage[pl.ds(k * chunks + c, sources, stride=capacity * chunks), :] = out[
                k * sources : (k + 1) * sources, c * LANES : (c + 1) * LANES
            ]
    out_ref[...] = stage[...].astype(jnp.bfloat16)


def add_kernel(index, arrived_ref, part_ref, out_ref):
    out_ref[...] = (
        arrived_ref[...].astype(jnp.float32) + part_ref[index].astype(jnp.float32)
    ).astype(jnp.bfloat16)


def mix_kernel(experts, capacity, routes_ref, gates_ref, back_ref, out_ref, stage):
    width = out_ref.shape[1]
    chunks = width // LANES
    block = capacity * chunks
    stage[...] = back_ref[...].astype(jnp.float32)
    picks = slot_picks(routes_ref, experts, capacity)
    gates = [jnp.sum(pick * gates_ref[...], axis=1, keepdims=True) for pick in picks]
    picks = jnp.concatenate(picks, axis=0).astype(jnp.bfloat16)
    for c in range(chunks):
        scaled = [
            (gates[k] * stage[pl.ds(k * chunks + c, experts, stride=block), :]).astype(jnp.bfloat16)
            for k in range(capacity)
        ]
        out_ref[:, c * LANES : (c + 1) * LANES] = lax.dot_general(
            picks,
            jnp.concatenate(scaled, axis=0),
            (((0,), (0,)), ((), ())),
            preferred_element_type=jnp.float32,
        ).astype(jnp.bfloat16)


def call(kernel, out_shape, scratch, flops, moved, smem=(), hbm=(), out_hbm=False):
    def spec(i):
        space = pltpu.SMEM if i in smem else pltpu.HBM if i in hbm else pltpu.VMEM
        return pl.BlockSpec(memory_space=space)

    out_space = pltpu.HBM if out_hbm else pltpu.VMEM

    def run(*args):
        args = [
            pltpu.with_memory_space_constraint(a, pltpu.HBM) if i in hbm else a
            for i, a in enumerate(args)
        ]
        return pl.pallas_call(
            kernel,
            out_shape=out_shape,
            in_specs=[spec(i) for i in range(len(args))],
            out_specs=jax.tree.map(lambda _: pl.BlockSpec(memory_space=out_space), out_shape),
            scratch_shapes=scratch,
            compiler_params=pltpu.CompilerParams(vmem_limit_bytes=VMEM_LIMIT),
            cost_estimate=pl.CostEstimate(flops=flops, bytes_accessed=moved, transcendentals=0),
        )(*args)

    return run


def on_device(latent, cotangent, routes, gates, up_weight, down_weight):
    experts = lax.axis_size("expert")
    groups = lax.axis_size("y") * lax.axis_size("core")
    tokens, width = latent.shape
    hidden_width = up_weight.shape[2]
    capacity = max(2, 3 * tokens // (2 * experts))
    slots = experts * capacity
    chunks = width // LANES
    factor = 1.0 / (tokens * groups) ** 0.5
    bf16 = functools.partial(jax.ShapeDtypeStruct, dtype=jnp.bfloat16)
    f32 = lambda *shape: pltpu.VMEM(shape, jnp.float32)
    half = lambda *shape: pltpu.VMEM(shape, jnp.bfloat16)
    route_row, gate_row = routes.reshape(1, tokens), gates.reshape(1, tokens)

    sems = lambda n: pltpu.SemaphoreType.DMA((n,))
    sent = call(
        functools.partial(pack_kernel, experts, capacity),
        bf16((2 * slots * chunks, LANES)),
        [
            f32(2 * slots * chunks, LANES),
            pltpu.VMEM((1, tokens), jnp.int32),
            f32(1, tokens),
            half(tokens, width),
            half(tokens, width),
            sems(4),
        ],
        4 * slots * tokens * width,
        4 * tokens * width + 4 * slots * width,
        hbm=(0, 1, 2, 3),
    )(route_row, gate_row, latent, cotangent)
    received = lax.all_to_all(
        sent.reshape(experts, -1, LANES), "expert", split_axis=0, concat_axis=0, tiled=True
    ).reshape(-1, LANES)
    other = lax.ppermute(received, "core", [(i, CORES - 1 - i) for i in range(CORES)])
    hidden, cots, up = call(
        functools.partial(hidden_kernel, experts, capacity),
        (
            bf16((slots, hidden_width)),
            bf16((slots, width)),
            bf16((width, hidden_width)),
        ),
        [
            f32(2 * slots * chunks, LANES),
            half(slots, width),
            sems(hidden_width // (4 * LANES)),
        ],
        2 * slots * width * hidden_width,
        2 * width * hidden_width + 6 * slots * width + 2 * slots * hidden_width,
        hbm=(1,),
    )(received, up_weight[0])
    ring = lax.axis_size("y")
    far, near = ring // 2, (ring - 1) // 2
    place = jnp.stack([lax.axis_index("y"), lax.axis_index("core"), ring]).astype(jnp.int32)
    block = (hidden_width // (ring * CORES), width)
    firsts = (far, ring - near)
    rest = tuple(i for i in range(ring) if i not in firsts)
    upward, downward, parts, down = call(
        functools.partial(grad_kernel, experts, capacity, factor, firsts + rest),
        (
            bf16(block),
            bf16(block),
            bf16((len(rest),) + block),
            bf16((hidden_width, width)),
        ),
        [
            f32(2 * slots * chunks, LANES),
            half(slots, width),
            half(CORES * slots, width),
            half(CORES * slots, hidden_width // CORES),
            pltpu.SemaphoreType.DMA,
        ],
        3 * slots * width * hidden_width,
        2 * width * hidden_width + 8 * slots * width,
        smem=(0,),
        hbm=(5,),
    )(place, hidden, cots, other, up, down_weight[0])
    out = call(
        functools.partial(down_kernel, experts, capacity),
        bf16((slots * chunks, LANES)),
        [f32(slots * chunks, LANES)],
        2 * slots * width * hidden_width,
        2 * width * hidden_width + 4 * slots * width,
    )(hidden, down)
    after, before = (
        [
            (i * CORES + core, (i + (step if core == 0 else -step)) % ring * CORES + core)
            for i in range(ring)
            for core in range(CORES)
        ]
        for step in (1, -1)
    )

    def add(arrived, offset):
        return call(
            functools.partial(add_kernel, rest.index(offset)),
            bf16(block),
            [],
            ADD_WEIGHT * block[0] * block[1],
            6 * block[0] * block[1],
        )(arrived, parts)

    total = parts[rest.index(0)]
    for hop in range(far):
        upward = lax.ppermute(upward, ("y", "core"), after)
        if hop == 0:
            upward, downward = lax.optimization_barrier((upward, downward))
        if hop < far - 1:
            upward = add(upward, far - 1 - hop)
    for hop in range(near):
        downward = lax.ppermute(downward, ("y", "core"), before)
        if hop < near - 1:
            downward = add(downward, ring - near + 1 + hop)
    returned = lax.all_to_all(
        out.reshape(experts, -1, LANES), "expert", split_axis=0, concat_axis=0, tiled=True
    ).reshape(-1, LANES)
    mixed = call(
        functools.partial(mix_kernel, experts, capacity),
        bf16((tokens, width)),
        [f32(slots * chunks, LANES)],
        2 * slots * tokens * width,
        2 * slots * width + 2 * tokens * width,
    )(route_row, gate_row, returned)
    mixed, upward, downward = lax.optimization_barrier((mixed, upward, downward))
    down_grad = sum(term.astype(jnp.float32) for term in (total, upward, downward)).astype(
        jnp.bfloat16
    )
    return mixed, down_grad[None]


def solution(mesh):
    experts, groups = mesh.devices.shape
    split = Mesh(mesh.devices.reshape(experts, groups // CORES, CORES), ("expert", "y", "core"))
    rows = P(("expert", "y", "core"), None)
    weights = P("expert", None, None)
    return jax.shard_map(
        on_device,
        mesh=split,
        in_specs=(rows, rows, rows, rows, weights, weights),
        out_specs=(rows, P("expert", ("y", "core"), None)),
        check_vma=False,
    )
```

```python
import functools

import jax
import jax.numpy as jnp
from jax import lax
from jax.experimental import pallas as pl
from jax.experimental.pallas import tpu as pltpu
from jax.sharding import Mesh, PartitionSpec as P

LANES = 128
ADD_WEIGHT = 20000
CORES = 2
VMEM_LIMIT = 24 * 1024 * 1024


def slot_picks(routes_ref, experts, capacity):
    tokens = routes_ref.shape[1]
    named = routes_ref[...] == lax.broadcasted_iota(jnp.int32, (experts, tokens), 0)
    earlier = lax.broadcasted_iota(jnp.int32, (tokens, tokens), 0) < lax.broadcasted_iota(
        jnp.int32, (tokens, tokens), 1
    )
    rank = jnp.dot(
        jnp.where(named, 1.0, 0.0).astype(jnp.bfloat16),
        jnp.where(earlier, 1.0, 0.0).astype(jnp.bfloat16),
        preferred_element_type=jnp.float32,
    )
    return [
        jnp.where(jnp.logical_and(named, rank == float(k)), 1.0, 0.0) for k in range(capacity)
    ]


def pack_kernel(
    experts, capacity, routes_hbm, gates_hbm, latent_hbm, cot_hbm, out_ref, stage, routes, gates, latent, cot, sems
):
    copies = [
        pltpu.make_async_copy(source, target, sems.at[i])
        for i, (source, target) in enumerate(
            ((routes_hbm, routes), (gates_hbm, gates), (latent_hbm, latent), (cot_hbm, cot))
        )
    ]
    for copy in copies:
        copy.start()
    chunks = latent.shape[1] // LANES
    block = 2 * capacity * chunks
    copies[0].wait()
    copies[1].wait()
    picks = slot_picks(routes, experts, capacity)
    for part, source in enumerate((latent, cot)):
        copies[2 + part].wait()
        for k, pick in enumerate(picks):
            rows = jnp.dot(
                pick.astype(jnp.bfloat16), source[...], preferred_element_type=jnp.float32
            )
            if part == 1:
                rows = rows * jnp.sum(pick * gates[...], axis=1, keepdims=True)
            for c in range(chunks):
                first = (2 * k + part) * chunks + c
                stage[pl.ds(first, experts, stride=block), :] = rows[:, c * LANES : (c + 1) * LANES]
    out_ref[...] = stage[...].astype(jnp.bfloat16)


def unpack(stage, out_ref, at, sources, capacity, parts, part):
    chunks = out_ref.shape[1] // LANES
    block = parts * capacity * chunks
    for k in range(capacity):
        for c in range(chunks):
            out_ref[at + k * sources : at + (k + 1) * sources, c * LANES : (c + 1) * LANES] = stage[
                pl.ds((parts * k + part) * chunks + c, sources, stride=block), :
            ].astype(jnp.bfloat16)


def activation(rows, weight):
    preact = jnp.dot(rows, weight, preferred_element_type=jnp.float32)
    return (jnp.maximum(preact, 0.0) ** 2).astype(jnp.bfloat16)


def hidden_kernel(
    sources, capacity, recv_ref, up_hbm, hidden_ref, cots_ref, up_ref, stage, rows, sems
):
    tile = 4 * LANES
    columns = [pl.ds(j * tile, tile) for j in range(up_ref.shape[1] // tile)]
    copies = [
        pltpu.make_async_copy(up_hbm.at[:, at], up_ref.at[:, at], sems.at[j])
        for j, at in enumerate(columns)
    ]
    for copy in copies:
        copy.start()
    stage[...] = recv_ref[...].astype(jnp.float32)
    unpack(stage, rows, 0, sources, capacity, 2, 0)
    unpack(stage, cots_ref, 0, sources, capacity, 2, 1)
    for copy, at in zip(copies, columns):
        copy.wait()
        hidden_ref[:, at] = activation(rows[...], up_ref[:, at])


def grad_kernel(
    sources,
    capacity,
    factor,
    offsets,
    place_ref,
    hidden_ref,
    own_cots_ref,
    other_ref,
    up_ref,
    down_hbm,
    up_block_ref,
    down_block_ref,
    part_ref,
    down_ref,
    stage,
    rows,
    cots,
    acts,
    sem,
):
    fetch = pltpu.make_async_copy(down_hbm, down_ref, sem)
    fetch.start()
    slots = sources * capacity
    stage[...] = other_ref[...].astype(jnp.float32)
    unpack(stage, rows, 0, sources, capacity, 2, 0)
    unpack(stage, cots, slots, sources, capacity, 2, 1)
    cots[:slots, :] = own_cots_ref[...]
    for j in range(0, len(offsets), 4):
        columns = []
        for offset in offsets[j : j + 4]:
            turn = jnp.where(place_ref[1] == 0, offset, place_ref[2] - offset)
            y = lax.rem(place_ref[0] + turn, place_ref[2])
            columns.append(pl.ds(pl.multiple_of((CORES * y + place_ref[1]) * LANES, LANES), LANES))
        at = pl.ds(j * LANES, 4 * LANES)
        weight = jnp.concatenate([up_ref[:, column] for column in columns], axis=1)
        acts[:slots, at] = jnp.concatenate([hidden_ref[:, column] for column in columns], axis=1)
        acts[slots:, at] = activation(rows[...], weight)
    product = lax.dot_general(
        acts[...], cots[...], (((0,), (0,)), ((), ())), preferred_element_type=jnp.float32
    )
    product = (factor * product).astype(jnp.bfloat16)
    up_block_ref[...] = product[:LANES]
    down_block_ref[...] = product[LANES : 2 * LANES]
    for j in range(len(offsets) - 2):
        part_ref[j] = product[(j + 2) * LANES : (j + 3) * LANES]
    fetch.wait()


def down_kernel(sources, capacity, hidden_ref, down_ref, out_ref, stage):
    width = down_ref.shape[1]
    chunks = width // LANES
    out = jnp.dot(hidden_ref[...], down_ref[...], preferred_element_type=jnp.float32)
    for k in range(capacity):
        for c in range(chunks):
            stage[pl.ds(k * chunks + c, sources, stride=capacity * chunks), :] = out[
                k * sources : (k + 1) * sources, c * LANES : (c + 1) * LANES
            ]
    out_ref[...] = stage[...].astype(jnp.bfloat16)


def add_kernel(index, arrived_ref, part_ref, out_ref):
    out_ref[...] = (
        arrived_ref[...].astype(jnp.float32) + part_ref[index].astype(jnp.float32)
    ).astype(jnp.bfloat16)


def mix_kernel(experts, capacity, routes_ref, gates_ref, back_ref, out_ref, stage):
    width = out_ref.shape[1]
    chunks = width // LANES
    block = capacity * chunks
    stage[...] = back_ref[...].astype(jnp.float32)
    picks = slot_picks(routes_ref, experts, capacity)
    gates = [jnp.sum(pick * gates_ref[...], axis=1, keepdims=True) for pick in picks]
    picks = jnp.concatenate(picks, axis=0).astype(jnp.bfloat16)
    for c in range(chunks):
        scaled = [
            (gates[k] * stage[pl.ds(k * chunks + c, experts, stride=block), :]).astype(jnp.bfloat16)
            for k in range(capacity)
        ]
        out_ref[:, c * LANES : (c + 1) * LANES] = lax.dot_general(
            picks,
            jnp.concatenate(scaled, axis=0),
            (((0,), (0,)), ((), ())),
            preferred_element_type=jnp.float32,
        ).astype(jnp.bfloat16)


def call(kernel, out_shape, scratch, flops, moved, smem=(), hbm=(), out_hbm=False):
    def spec(i):
        space = pltpu.SMEM if i in smem else pltpu.HBM if i in hbm else pltpu.VMEM
        return pl.BlockSpec(memory_space=space)

    out_space = pltpu.HBM if out_hbm else pltpu.VMEM

    def run(*args):
        args = [
            pltpu.with_memory_space_constraint(a, pltpu.HBM) if i in hbm else a
            for i, a in enumerate(args)
        ]
        return pl.pallas_call(
            kernel,
            out_shape=out_shape,
            in_specs=[spec(i) for i in range(len(args))],
            out_specs=jax.tree.map(lambda _: pl.BlockSpec(memory_space=out_space), out_shape),
            scratch_shapes=scratch,
            compiler_params=pltpu.CompilerParams(vmem_limit_bytes=VMEM_LIMIT),
            cost_estimate=pl.CostEstimate(flops=flops, bytes_accessed=moved, transcendentals=0),
        )(*args)

    return run


def on_device(latent, cotangent, routes, gates, up_weight, down_weight):
    experts = lax.axis_size("expert")
    groups = lax.axis_size("y") * lax.axis_size("core")
    tokens, width = latent.shape
    hidden_width = up_weight.shape[2]
    capacity = max(2, 3 * tokens // (2 * experts))
    slots = experts * capacity
    chunks = width // LANES
    factor = 1.0 / (tokens * groups) ** 0.5
    bf16 = functools.partial(jax.ShapeDtypeStruct, dtype=jnp.bfloat16)
    f32 = lambda *shape: pltpu.VMEM(shape, jnp.float32)
    half = lambda *shape: pltpu.VMEM(shape, jnp.bfloat16)
    route_row, gate_row = routes.reshape(1, tokens), gates.reshape(1, tokens)

    sems = lambda n: pltpu.SemaphoreType.DMA((n,))
    sent = call(
        functools.partial(pack_kernel, experts, capacity),
        bf16((2 * slots * chunks, LANES)),
        [
            f32(2 * slots * chunks, LANES),
            pltpu.VMEM((1, tokens), jnp.int32),
            f32(1, tokens),
            half(tokens, width),
            half(tokens, width),
            sems(4),
        ],
        4 * slots * tokens * width,
        4 * tokens * width + 4 * slots * width,
        hbm=(0, 1, 2, 3),
    )(route_row, gate_row, latent, cotangent)
    received = lax.all_to_all(
        sent.reshape(experts, -1, LANES), "expert", split_axis=0, concat_axis=0, tiled=True
    ).reshape(-1, LANES)
    other = lax.ppermute(received, "core", [(i, CORES - 1 - i) for i in range(CORES)])
    hidden, cots, up = call(
        functools.partial(hidden_kernel, experts, capacity),
        (
            bf16((slots, hidden_width)),
            bf16((slots, width)),
            bf16((width, hidden_width)),
        ),
        [
            f32(2 * slots * chunks, LANES),
            half(slots, width),
            sems(hidden_width // (4 * LANES)),
        ],
        2 * slots * width * hidden_width,
        2 * width * hidden_width + 6 * slots * width + 2 * slots * hidden_width,
        hbm=(1,),
    )(received, up_weight[0])
    ring = lax.axis_size("y")
    far, near = ring // 2, (ring - 1) // 2
    place = jnp.stack([lax.axis_index("y"), lax.axis_index("core"), ring]).astype(jnp.int32)
    block = (hidden_width // (ring * CORES), width)
    firsts = (far, ring - near)
    rest = tuple(i for i in range(ring) if i not in firsts)
    upward, downward, parts, down = call(
        functools.partial(grad_kernel, experts, capacity, factor, firsts + rest),
        (
            bf16(block),
            bf16(block),
            bf16((len(rest),) + block),
            bf16((hidden_width, width)),
        ),
        [
            f32(2 * slots * chunks, LANES),
            half(slots, width),
            half(CORES * slots, width),
            half(CORES * slots, hidden_width // CORES),
            pltpu.SemaphoreType.DMA,
        ],
        3 * slots * width * hidden_width,
        2 * width * hidden_width + 8 * slots * width,
        smem=(0,),
        hbm=(5,),
    )(place, hidden, cots, other, up, down_weight[0])
    out = call(
        functools.partial(down_kernel, experts, capacity),
        bf16((slots * chunks, LANES)),
        [f32(slots * chunks, LANES)],
        2 * slots * width * hidden_width,
        2 * width * hidden_width + 4 * slots * width,
    )(hidden, down)
    after, before = (
        [
            (i * CORES + core, (i + (step if core == 0 else -step)) % ring * CORES + core)
            for i in range(ring)
            for core in range(CORES)
        ]
        for step in (1, -1)
    )

    def add(arrived, offset):
        return call(
            functools.partial(add_kernel, rest.index(offset)),
            bf16(block),
            [],
            ADD_WEIGHT * block[0] * block[1],
            6 * block[0] * block[1],
        )(arrived, parts)

    total = parts[rest.index(0)]
    for hop in range(far):
        upward = lax.ppermute(upward, ("y", "core"), after)
        if hop < near:
            downward = lax.ppermute(downward, ("y", "core"), before)
        if hop < far - 1:
            upward = add(upward, far - 1 - hop)
        if hop < near - 1:
            downward = add(downward, ring - near + 1 + hop)
    returned = lax.all_to_all(
        out.reshape(experts, -1, LANES), "expert", split_axis=0, concat_axis=0, tiled=True
    ).reshape(-1, LANES)
    mixed = call(
        functools.partial(mix_kernel, experts, capacity),
        bf16((tokens, width)),
        [f32(slots * chunks, LANES)],
        2 * slots * tokens * width,
        2 * slots * width + 2 * tokens * width,
    )(route_row, gate_row, returned)
    mixed, upward, downward = lax.optimization_barrier((mixed, upward, downward))
    down_grad = sum(term.astype(jnp.float32) for term in (total, upward, downward)).astype(
        jnp.bfloat16
    )
    return mixed, down_grad[None]


def solution(mesh):
    experts, groups = mesh.devices.shape
    split = Mesh(mesh.devices.reshape(experts, groups // CORES, CORES), ("expert", "y", "core"))
    rows = P(("expert", "y", "core"), None)
    weights = P("expert", None, None)
    return jax.shard_map(
        on_device,
        mesh=split,
        in_specs=(rows, rows, rows, rows, weights, weights),
        out_specs=(rows, P("expert", ("y", "core"), None)),
        check_vma=False,
    )
```
